32 devices in a mesh: groups: 2 (over y), seq: 4 (over z), beam: 4 (over x, core).
Axes of the slice: x: 2, y: 2, z: 4, core: 2. Of those that a mesh axis runs over, the one named last changes fastest.
Arguments:
- prompt_values: bfloat16 [2048, 8192], P(('groups', 'seq'), 'beam'), parts along dimension 0, may hold values from -6 to 6
- prompt_keys: bfloat16 [2048, 128], P(('groups', 'seq')), parts along dimension 0, may hold values from -0.31445312 to 0.31445312
- prompt_queries: bfloat16 [2048, 128], P(('groups', 'seq')), parts along dimension 0, may hold values from -0.31445312 to 0.31445312
- logarithm_state_decay: float32 [2048, 128], P(('groups', 'seq'), 'beam'), parts along dimension 0, may hold values from -1 to 0
- step_values: bfloat16 [8, 4, 8192], P('groups', 'beam', 'seq'), parts along dimension 0, may hold values from -6 to 6
- step_keys: bfloat16 [8, 4, 128], P('groups', 'beam'), parts along dimension 0, may hold values from -6 to 6
- step_queries: bfloat16 [8, 4, 128], P('groups', 'beam'), parts along dimension 0, may hold values from -0.31445312 to 0.31445312
- step_decay: float32 [8, 4, 128], P('groups', 'beam', 'seq'), parts along dimension 0, may hold values from -0.6 to -0.02
- step_logprob: float32 [8, 4], P('groups', 'beam'), parts along dimension 0, may hold values from -6 to -0.05
- parents: int32 [8, 4], P('groups', 'beam'), parts along dimension 0, may hold values from 0 to 3
- finished: int32 [8, 4], P('groups', 'beam'), parts along dimension 0, may hold values 0 or 1
- lengths: int32 [8], P(('groups', 'beam')), parts along dimension 0, may hold values from 1 to 59
- init_score: float32 [8], P(('groups', 'beam')), parts along dimension 0, may hold values from -20 to -2
Outputs:
- prompt_output: bfloat16 [2048, 8192], P(('groups', 'seq'), 'beam'), parts along dimension 0
- step_output: bfloat16 [8, 4, 8192], P('groups', 'beam', 'seq'), parts along dimension 0
- ranked: float32 [8, 4], P('groups', 'beam'), parts along dimension 0
- beam_states: float32 [8, 8192, 128], P(('groups', 'beam'), 'seq'), parts along dimension 0
The draws below stay inside these ranges and needn't reach their ends.
There are 2 independent parts, one for each index of `groups`. The reference program is written for one: setup_inputs(seed, part) draws one part's arguments, and reference() takes and returns one part's arrays. A program takes and returns all parts, laid end to end along the dimension named above; each array names one. Nothing has to cross between parts.
All inputs are finite; a program needn't handle non-finite values. No bound on the sum of `finished` on one device may be relied on, other than what follows from the above.
Results may differ from the reference program's by a relative error of at most 0.0056.
Values sent between devices are 32-bit elements; how exact they have to be, the bound alone decides.
A program may use at most 64 MiB of HBM per device.

```python
import math
import jax
import jax.numpy as jnp
from jax import lax

H = 128
P_SIZE = 64
N = 128
STEPS = 4
TOK_DEV = 256
SPAN = 256
TOKENS = 1024
BEAMS = 4


def draw_logarithm_state_decay(key, part):
    keys = jax.random.split(jax.random.fold_in(key, 11), 7)
    slow_share = 0.5
    slow = jax.random.uniform(keys[0], (H,)) < slow_share
    slow_rate = jnp.exp(jax.random.uniform(keys[1], (H,), minval=math.log(0.05 / TOKENS), maxval=math.log(0.5 / TOKENS)))
    fast_rate = jnp.exp(jax.random.uniform(keys[2], (H,), minval=math.log(2.0 / TOKENS), maxval=math.log(1.0 / 30.0)))
    head_rate = jnp.where(slow, slow_rate, fast_rate)
    token_multiplier = jnp.exp(jax.random.uniform(keys[3], (TOKENS // TOK_DEV, TOK_DEV, H), minval=-math.log(2.0), maxval=math.log(2.0)))
    block_factor = jnp.exp(jax.random.uniform(keys[4], (TOKENS // TOK_DEV, 1, H), minval=-math.log(2.0), maxval=math.log(2.0)))
    gentle_portion = (head_rate[None, None, :] * token_multiplier * block_factor).reshape(TOKENS, H)
    spots = jax.random.randint(keys[5], (3,), 0, TOKENS)
    objective_entries = jax.random.uniform(keys[6], (3, H), minval=0.22, maxval=0.5)
    agreement_occurrences = (jnp.arange(TOKENS)[:, None] == spots[None, :]).astype(jnp.float32)
    spike_occurrences = jnp.dot(agreement_occurrences, objective_entries)
    return (-gentle_portion - spike_occurrences).astype(jnp.float32)


def with_ends(array, stream_key, low, top_value):
    place = [jax.random.randint(jax.random.fold_in(stream_key, axis), (), 0, length) for axis, length in enumerate(array.shape)]
    main_axis = array.shape.index(max(array.shape))
    neighbour = place[:main_axis] + [(place[main_axis] + 1) % array.shape[main_axis]] + place[main_axis + 1:]
    return array.at[tuple(place)].set(low).at[tuple(neighbour)].set(top_value)


def shard_levels(rng, dims, cuts, smallest, largest):
    gain, own = 1.0, jax.random.fold_in(rng, 6)
    for dim, shards_of in cuts:
        draws = jnp.exp(jax.random.uniform(jax.random.fold_in(own, dim), (shards_of,), jnp.float32, smallest / len(cuts), largest / len(cuts)))
        gain = gain * jnp.repeat(draws, dims[dim] // shards_of).reshape([-1 if axis == dim else 1 for axis in range(len(dims))])
    return gain


def scatter_about(stream_key, shape, scale, reach, pieces=(), held_as=jnp.bfloat16):
    drawn = jax.random.normal(stream_key, shape, jnp.float32) * scale
    if len(pieces) > 0:
        drawn = shard_levels(stream_key, shape, pieces, -0.22, 0.18) * drawn
    return jnp.clip(drawn, min=-reach, max=reach).astype(held_as)


def setup_inputs(seed: int = 0, part: int = 0) -> dict:
    streams_of = jax.random.split(jax.random.key(seed), 14)
    part_keys = jax.random.split(jax.random.fold_in(streams_of[13], part), 14)
    prompt_values = scatter_about(part_keys[0], (TOKENS, H * P_SIZE), 1.0, 6.0, ((0, 4), (1, 4)))
    prompt_keys = scatter_about(part_keys[1], (TOKENS, N), ((N * TOKENS) ** -0.25), 0.31445312, ((0, 4),))
    prompt_queries = scatter_about(part_keys[2], (TOKENS, N), ((N * TOKENS) ** -0.25), 0.31445312, ((0, 4),))
    logarithm_state_decay = draw_logarithm_state_decay(jax.random.fold_in(jax.random.fold_in(streams_of[13], part), 71), part)
    step_values = scatter_about(part_keys[4], (STEPS, BEAMS, H * P_SIZE), 1.0, 6.0, ((1, 4), (2, 4)))
    step_keys = scatter_about(part_keys[5], (STEPS, BEAMS, N), 1.0, 6.0, ((1, 4),))
    step_queries = scatter_about(part_keys[6], (STEPS, BEAMS, N), ((N * TOKENS) ** -0.25), 0.31445312, ((1, 4),))
    step_decay = jnp.clip(-0.6 + 0.58000002 * jax.random.uniform(part_keys[7], (STEPS, BEAMS, H), jnp.float32) ** shard_levels(part_keys[7], (STEPS, BEAMS, H), ((1, 4), (2, 4)), -0.2, 0.2), -0.6, -0.02)
    step_logprob = jnp.clip(-6.0 + 5.95 * jax.random.uniform(part_keys[8], (STEPS, BEAMS), jnp.float32) ** shard_levels(part_keys[8], (STEPS, BEAMS), ((1, 4),), -0.2, 0.2), -6.0, -0.05)
    parents = with_ends(jax.random.randint(part_keys[9], (STEPS, BEAMS), 0, BEAMS), jax.random.fold_in(part_keys[9], 1), 0, BEAMS - 1).astype(jnp.int32)
    finished = with_ends((jax.random.randint(part_keys[10], (STEPS, BEAMS), 0, 3) < 1).astype(jnp.int32), jax.random.fold_in(part_keys[10], 1), 0, 1)
    lengths = with_ends(jax.random.randint(part_keys[11], (BEAMS,), 1, 60), jax.random.fold_in(part_keys[11], 1), 1, 59).astype(jnp.int32)
    init_score = jnp.clip(-20.0 + 18.0 * jax.random.uniform(part_keys[12], (BEAMS,), jnp.float32) ** shard_levels(part_keys[12], (BEAMS,), ((0, 4),), -0.2, 0.2), -20.0, -2.0)
    return {"prompt_values": prompt_values, "prompt_keys": prompt_keys, "prompt_queries": prompt_queries, "logarithm_state_decay": logarithm_state_decay, "step_values": step_values, "step_keys": step_keys, "step_queries": step_queries, "step_decay": step_decay, "step_logprob": step_logprob, "parents": parents, "finished": finished, "lengths": lengths, "init_score": init_score}


def reference(prompt_values, prompt_keys, prompt_queries, logarithm_state_decay, step_values, step_keys, step_queries, step_decay, step_logprob, parents, finished, lengths, init_score):
    block_count = TOKENS // SPAN
    values_blocks = prompt_values.reshape(block_count, SPAN, H, P_SIZE)
    keys_blocks = prompt_keys.reshape(block_count, SPAN, N)
    query_blocks = prompt_queries.reshape(block_count, SPAN, N)
    decay_blocks = logarithm_state_decay.reshape(block_count, SPAN, H)
    lower = jnp.tril(jnp.ones((SPAN, SPAN), dtype=bool))

    def block_step(state_now, item):
        values_one, keys_one, query_one, single_token_decay = item
        sums_one = jnp.cumsum(single_token_decay, axis=0)
        scores = jnp.dot(query_one, keys_one.T, preferred_element_type=jnp.float32)
        spread = jnp.where(lower[:, :, None], sums_one[:, None, :] - sums_one[None, :, :], -jnp.inf)
        weights = (scores[:, :, None] * jnp.exp(spread)).astype(jnp.bfloat16)
        inner = jnp.einsum("ijh,jhp->ihp", weights.astype(jnp.float32), values_one.astype(jnp.float32))
        rounded = state_now.astype(jnp.bfloat16).astype(jnp.float32)
        carried = jnp.einsum("in,hpn->ihp", query_one.astype(jnp.float32), rounded) * jnp.exp(sums_one)[:, :, None]
        output_one = (inner + carried).astype(jnp.bfloat16).reshape(SPAN, H * P_SIZE)
        tail_decay = jnp.exp(sums_one[-1:, :] - sums_one)
        scaled = (values_one.astype(jnp.float32) * tail_decay[:, :, None]).astype(jnp.bfloat16)
        block_state = jnp.einsum("jhp,jn->hpn", scaled.astype(jnp.float32), keys_one.astype(jnp.float32))
        following_memory = jnp.exp(sums_one[-1])[:, None, None] * state_now + block_state
        return following_memory, output_one

    final_state, outputs = lax.scan(block_step, jnp.zeros((H, P_SIZE, N), jnp.float32), (values_blocks, keys_blocks, query_blocks, decay_blocks))
    prompt_output = outputs.reshape(TOKENS, H * P_SIZE)

    state_all = jnp.broadcast_to(final_state[None], (BEAMS, H, P_SIZE, N))
    score_all = init_score
    length_all = lengths.astype(jnp.float32)
    step_list = []
    ranked_list = []
    for step_index in range(STEPS):
        parent_now = parents[step_index]
        state_all = state_all[parent_now]
        score_all = score_all[parent_now]
        length_all = length_all[parent_now]
        done = finished[step_index] == 1
        live = (1 - finished[step_index]).astype(jnp.float32)
        values_now = step_values[step_index].astype(jnp.float32).reshape(BEAMS, H, P_SIZE)
        keys_now = step_keys[step_index].astype(jnp.float32)
        updated = jnp.exp(step_decay[step_index])[:, :, None, None] * state_all + values_now[:, :, :, None] * keys_now[:, None, None, :]
        state_all = jnp.where(done[:, None, None, None], state_all, updated)
        rounded = state_all.astype(jnp.bfloat16).astype(jnp.float32)
        output_now = jnp.einsum("bhpn,bn->bhp", rounded, step_queries[step_index].astype(jnp.float32))
        output_now = jnp.where(done[:, None, None], jnp.float32(0.0), output_now)
        step_list.append(output_now.reshape(BEAMS, H * P_SIZE).astype(jnp.bfloat16))
        score_all = score_all + live * step_logprob[step_index]
        length_all = length_all + live
        normed = score_all / ((5.0 + length_all) / 6.0) ** 0.6
        ranked_list.append(normed - jnp.max(normed))
    step_output = jnp.stack(step_list)
    ranked = jnp.stack(ranked_list)
    beam_states = state_all.reshape(BEAMS, H * P_SIZE, N)
    return prompt_output, step_output, ranked, beam_states
```

```python
import functools
import math

import jax
import jax.numpy as jnp
from jax import lax
from jax.experimental import pallas as pl
from jax.experimental.pallas import tpu as pltpu
from jax.sharding import PartitionSpec as P

P_SIZE = 64
LANES = 128
PAIR = LANES // P_SIZE
ROWS = 8
LAG = 2
LOG2E = math.log2(math.e)
MESH = pl.DeviceIdType.MESH
F32 = jnp.float32
BF16 = jnp.bfloat16


def split3(x):
    first = x.astype(BF16)
    rest = x - first.astype(F32)
    second = rest.astype(BF16)
    return first, second, (rest - second.astype(F32)).astype(BF16)


def mm(a, b):
    return jnp.dot(a, b, preferred_element_type=F32)


def mm_first(a, b):
    return lax.dot_general(a, b, (((0,), (0,)), ((), ())), preferred_element_type=F32)


def kernel(
    ns,
    nb,
    x_ref,
    keys_ref,
    queries_ref,
    decay_ref,
    sv_ref,
    sk_ref,
    sq_ref,
    sd_ref,
    lp_ref,
    par_ref,
    fin_ref,
    len_ref,
    score_ref,
    out_ref,
    so_ref,
    rank_ref,
    beam_ref,
    sums_ref,
    keys_t,
    scores,
    own,
    inner_ref,
    up_recv,
    up_out,
    dn_recv,
    dn_out,
    final,
    vals,
    small,
    pad,
    dec_d,
    dec_add,
    dec_cv,
    dec_k,
    dec_q,
    up_ss,
    up_rs,
    dn_ss,
    dn_rs,
    f_ss,
    f_rs,
    v_ss,
    v_rs,
    m_ss,
    m_rs,
):
    g = lax.axis_index("groups")
    s = lax.axis_index("seq")
    b = lax.axis_index("beam")
    toks, width = x_ref.shape
    n = keys_ref.shape[1]
    chunks = width // LANES
    steps = sv_ref.shape[0]
    dwidth = sv_ref.shape[2]
    dheads = dwidth // P_SIZE
    dchunks = dwidth // LANES
    last = ns - 1

    barrier = pltpu.get_barrier_semaphore()

    def peer(i):
        return lax.rem(b + i, nb)

    @pl.when(s > 0)
    def _():
        pl.semaphore_signal(barrier, inc=1, device_id=(g, s - 1, b), device_id_type=MESH)

    @pl.when(s < last)
    def _():
        pl.semaphore_signal(barrier, inc=1, device_id=(g, s + 1, b), device_id_type=MESH)

    for i in range(1, nb):
        pl.semaphore_signal(barrier, inc=1, device_id=(g, s, peer(i)), device_id_type=MESH)

    def up_copy(src, k):
        return pltpu.make_async_remote_copy(
            src_ref=src,
            dst_ref=up_recv.at[k],
            send_sem=up_ss.at[k],
            recv_sem=up_rs.at[k],
            device_id=(g, lax.rem(s + 1, ns), b),
            device_id_type=MESH,
        )

    def dn_copy(src, k):
        return pltpu.make_async_remote_copy(
            src_ref=src,
            dst_ref=dn_recv.at[k],
            send_sem=dn_ss.at[k],
            recv_sem=dn_rs.at[k],
            device_id=(g, lax.rem(s + ns - 1, ns), b),
            device_id_type=MESH,
        )

    def f_copy(kk, i):
        return pltpu.make_async_remote_copy(
            src_ref=final.at[kk],
            dst_ref=final.at[kk],
            send_sem=f_ss.at[kk, i - 1],
            recv_sem=f_rs.at[kk],
            device_id=(g, s, peer(i)),
            device_id_type=MESH,
        )

    def v_copy(i):
        return pltpu.make_async_remote_copy(
            src_ref=vals.at[b],
            dst_ref=vals.at[b],
            send_sem=v_ss.at[i - 1],
            recv_sem=v_rs.at[i - 1],
            device_id=(g, s, peer(i)),
            device_id_type=MESH,
        )

    def m_copy(i):
        return pltpu.make_async_remote_copy(
            src_ref=small.at[b],
            dst_ref=small.at[b],
            send_sem=m_ss.at[i - 1],
            recv_sem=m_rs.at[i - 1],
            device_id=(g, s, peer(i)),
            device_id_type=MESH,
        )

    def target(k):
        return (b * chunks + k) // dchunks

    def place(k):
        return lax.rem(b * chunks + k, dchunks)

    row_id = lax.broadcasted_iota(jnp.int32, (toks, toks), 0)
    col_id = lax.broadcasted_iota(jnp.int32, (toks, toks), 1)
    upper = (row_id <= col_id).astype(F32).astype(BF16)
    parts = split3(decay_ref[...] * LOG2E)
    sums_ref[...] = sum(mm_first(part, upper) for part in reversed(parts))
    keys_t[...] = keys_ref[...].astype(F32).T.astype(BF16)

    left = lax.broadcasted_iota(jnp.int32, (1, LANES), 1) < P_SIZE

    def head_column(head):
        row = sums_ref[pl.ds(head, 1), :]
        return row, jnp.broadcast_to(row, (LANES, toks)).T

    def pair_columns(k):
        heads = [head_column(k * PAIR + j) for j in range(PAIR)]
        return heads, jnp.where(left, heads[0][1], heads[1][1])

    def lanes_of(k):
        return pl.ds(pl.multiple_of(k * LANES, LANES), LANES)

    def make_state(k, carry):
        _, column = pair_columns(k)
        end = column[toks - 1 : toks, :]
        scaled = (x_ref[:, lanes_of(k)].astype(F32) * jnp.exp2(end - column)).astype(BF16)
        own[k, 0:n, :] = mm(keys_t[...], scaled)
        own[k, n : n + ROWS, :] = jnp.broadcast_to(jnp.exp2(end), (ROWS, LANES))
        return carry

    live = (1 - fin_ref[...]).astype(F32)
    pad[...] = jnp.zeros_like(pad)
    pad[0:steps, 0:dheads] = sd_ref[:, 0, :] * live * LOG2E
    spread = (
        lax.broadcasted_iota(jnp.int32, (LANES, dwidth), 0)
        == lax.broadcasted_iota(jnp.int32, (LANES, dwidth), 1) // P_SIZE
    )
    spread = spread.astype(F32).astype(BF16)
    wide = sum(mm(part, spread) for part in reversed(split3(pad[...])))
    vals[b, 0:steps, :] = sv_ref[:, 0, :].astype(F32) * live
    vals[b, steps : 2 * steps, :] = wide[0:steps, :]
    small[b] = jnp.zeros(small.shape[1:], F32)
    small[b, 0:steps, :] = sk_ref[:, 0, :].astype(F32)
    shape = (steps, LANES)
    small[b, steps : 2 * steps, :] = jnp.broadcast_to(par_ref[...].astype(F32), shape)
    small[b, 2 * steps : 3 * steps, :] = jnp.broadcast_to(lp_ref[...] * live, shape)
    small[b, 3 * steps : 4 * steps, :] = jnp.broadcast_to(live, shape)
    small[b, 4 * steps : 4 * steps + 1, :] = jnp.broadcast_to(score_ref[...], (1, LANES))
    small[b, 4 * steps + 1 : 4 * steps + 2, :] = jnp.broadcast_to(len_ref[...].astype(F32), (1, LANES))

    make_state(0, 0)

    met = nb - 1 + jnp.where(s > 0, 1, 0) + jnp.where(s < last, 1, 0)
    pl.semaphore_wait(barrier, met)

    for i in range(1, nb):
        m_copy(i).start()
        v_copy(i).start()

    def first_sends(k):
        @pl.when((s == 0) & (s < last))
        def _():
            up_copy(own.at[k, pl.ds(0, n)], k).start()

        @pl.when((s == last) & (s > target(k)))
        def _():
            dn_copy(own.at[k], k).start()

    first_sends(0)

    def state_and_send(k, carry):
        make_state(k, 0)
        first_sends(k)
        return carry

    lax.fori_loop(1, chunks, state_and_send, 0)

    scores[...] = jnp.where(row_id >= col_id, mm(queries_ref[...], keys_t[...]), 0.0)

    for i in range(1, nb):
        m_copy(i).wait_recv()
        v_copy(i).wait_recv()

    dec_d[...] = jnp.zeros_like(dec_d)
    dec_add[...] = jnp.zeros_like(dec_add)
    dec_cv[...] = jnp.zeros_like(dec_cv)
    dec_k[...] = jnp.zeros_like(dec_k)
    dec_q[...] = jnp.zeros_like(dec_q)
    dec_q[0:steps, :] = sq_ref[:, 0, :].astype(F32)
    own_slot = [jnp.where(b == slot, jnp.ones((1, LANES), F32), 0.0) for slot in range(nb)]

    def pick(weights, ref, row):
        total = None
        for slot in range(nb):
            value = ref[slot, row : row + 1, :]
            weight = weights[slot] if value.shape[1] == LANES else weights[slot][:, 0:1]
            total = weight * value if total is None else total + weight * value
        return total

    for step in range(steps):
        chain = own_slot
        decay = jnp.zeros((1, dwidth), F32)
        added = jnp.zeros((1, dwidth), F32)
        query = dec_q[step : step + 1, :]
        for t in range(step, -1, -1):
            value = jnp.exp2(decay) * pick(chain, vals, t)
            key = pick(chain, small, t)
            added = added + jnp.sum(key * query, axis=1, keepdims=True) * value
            decay = decay + pick(chain, vals, steps + t)
            if step == steps - 1:
                high = value.astype(BF16).astype(F32)
                dec_cv[t : t + 1, :] = high
                dec_cv[ROWS + t : ROWS + t + 1, :] = value - high
                dec_k[t : t + 1, :] = key
                dec_k[ROWS + t : ROWS + t + 1, :] = key
            if t > 0:
                parent = pick(chain, small, steps + t)
                chain = [jnp.where(parent == float(slot), 1.0, 0.0) for slot in range(nb)]
        open_now = live[step : step + 1, :]
        dec_d[step : step + 1, :] = jnp.exp2(decay)
        dec_add[step : step + 1, :] = added * open_now

    score = [small[slot, 4 * steps : 4 * steps + 1, :] for slot in range(nb)]
    length = [small[slot, 4 * steps + 1 : 4 * steps + 2, :] for slot in range(nb)]
    for step in range(steps):
        new_score, new_length, normed = [], [], []
        for slot in range(nb):
            parent = small[slot, steps + step : steps + step + 1, :]
            picked_score, picked_length = score[0], length[0]
            for other in range(1, nb):
                picked_score = jnp.where(parent == float(other), score[other], picked_score)
                picked_length = jnp.where(parent == float(other), length[other], picked_length)
            new_score.append(picked_score + small[slot, 2 * steps + step : 2 * steps + step + 1, :])
            new_length.append(picked_length + small[slot, 3 * steps + step : 3 * steps + step + 1, :])
            normed.append(new_score[-1] / jnp.exp(0.6 * jnp.log((5.0 + new_length[-1]) / 6.0)))
        score, length = new_score, new_length
        best = functools.reduce(jnp.maximum, normed)
        mine = sum(own_slot[slot] * normed[slot] for slot in range(nb))
        rank_ref[step : step + 1, :] = (mine - best)[:, 0:1]

    def forward_down(k):
        dn_copy(dn_out.at[k], k).wait_recv()
        shrink = dn_recv[k, n : n + 1, :]
        dn_out[k, 0:n, :] = dn_recv[k, 0:n, :] + shrink * own[k, 0:n, :]
        dn_out[k, n : n + ROWS, :] = dn_recv[k, n : n + ROWS, :] * own[k, n : n + ROWS, :]
        dn_copy(dn_out.at[k], k).start()

    def finish(kk):
        at = lanes_of(kk)
        state = final[kk]
        read = mm(dec_q[...].astype(BF16), state.astype(BF16))
        keep = pad[:, 0:1]
        dec_add[:, at] = keep * (dec_d[:, at] * read) + dec_add[:, at]
        outer = mm_first(dec_cv[:, at].astype(BF16), dec_k[...].astype(BF16))
        rows = pl.ds(pl.multiple_of(kk * LANES, LANES), LANES)
        beam_ref[0, rows, :] = (state * dec_d[steps - 1 : steps, at]).T + outer

    def await_and_finish(kk):
        @pl.when(b != (s * dchunks) // chunks)
        def _():
            f_copy(kk, 1).wait_recv()

        finish(kk)

    pad[...] = jnp.zeros_like(pad)
    pad[0:steps, :] = jnp.broadcast_to(live, (steps, LANES))

    def body(k, carry):
        heads, column = pair_columns(k)
        values = x_ref[:, lanes_of(k)]
        for i in range(toks // LANES):
            at = slice(i * LANES, (i + 1) * LANES)
            until = (i + 1) * LANES
            made = []
            for row, col in heads:
                blocks = []
                for j in range(i + 1):
                    to = slice(j * LANES, (j + 1) * LANES)
                    gap = jnp.minimum(col[at, :] - row[:, to], 0.0)
                    blocks.append((scores[at, to] * jnp.exp2(gap)).astype(BF16))
                weights = blocks[0] if i == 0 else jnp.concatenate(blocks, axis=1)
                made.append(mm(weights, values[0:until, :]))
            inner_ref[at, :] = jnp.where(left, made[0], made[1])

        goes_down = (s > target(k)) & (s < last)

        @pl.when(goes_down & (2 * s >= ns))
        def _():
            forward_down(k)

        @pl.when(s == 0)
        def _():
            out_ref[:, lanes_of(k)] = inner_ref[...].astype(BF16)

        @pl.when(s > 0)
        def _():
            up_copy(up_out.at[k], k).wait_recv()

            @pl.when((s < last) | (s == target(k)))
            def _():
                up_out[k] = own[k, n : n + 1, :] * up_recv[k] + own[k, 0:n, :]

            @pl.when(s < last)
            def _():
                up_copy(up_out.at[k], k).start()

            carried = mm(queries_ref[...], up_recv[k].astype(BF16)) * jnp.exp2(column)
            out_ref[:, lanes_of(k)] = (inner_ref[...] + carried).astype(BF16)

        @pl.when(goes_down & (2 * s < ns))
        def _():
            forward_down(k)

        @pl.when(s == target(k))
        def _():
            kk = place(k)

            @pl.when(s == 0)
            def _():
                up_out[k] = own[k, 0:n, :]

            @pl.when(s < last)
            def _():
                dn_copy(dn_out.at[k], k).wait_recv()
                final[kk] = dn_recv[k, n : n + 1, :] * up_out[k] + dn_recv[k, 0:n, :]

            @pl.when(s == last)
            def _():
                final[kk] = up_out[k]

            for i in range(1, nb):
                f_copy(kk, i).start()

        if dchunks == chunks:

            @pl.when(k >= LAG)
            def _():
                await_and_finish(k - LAG)

        return carry

    lax.fori_loop(0, chunks, body, 0)

    def rest(kk, carry):
        await_and_finish(kk)
        return carry

    lax.fori_loop(max(chunks - LAG, 0) if dchunks == chunks else 0, dchunks, rest, 0)
    for step in range(steps):
        so_ref[step] = dec_add[step : step + 1, :].astype(BF16)

    for i in range(1, nb):
        m_copy(i).wait_send()
        v_copy(i).wait_send()

    def drain(k, carry):
        @pl.when(s < last)
        def _():
            up_copy(up_out.at[k], k).wait_send()

        @pl.when(s > target(k))
        def _():
            dn_copy(dn_out.at[k], k).wait_send()

        @pl.when(s == target(k))
        def _():
            for i in range(1, nb):
                f_copy(place(k), i).wait_send()

        return carry

    lax.fori_loop(0, chunks, drain, 0)


def on_device(ns, nb, *args):
    x, keys, queries, decay, sv, sk, sq, sd, lp, par, fin, lens, score = args
    toks, width = x.shape
    n = keys.shape[1]
    heads = decay.shape[1]
    steps, _, dwidth = sv.shape
    chunks, dchunks = width // LANES, dwidth // LANES
    small_rows = -(-(4 * steps + 2) // ROWS) * ROWS
    dma = pltpu.SemaphoreType.DMA
    spec = pl.BlockSpec(memory_space=pltpu.VMEM)
    peers = max(nb - 1, 1)
    return pl.pallas_call(
        functools.partial(kernel, ns, nb),
        out_shape=(
            jax.ShapeDtypeStruct((toks, width), BF16),
            jax.ShapeDtypeStruct((steps, 1, dwidth), BF16),
            jax.ShapeDtypeStruct((steps, 1), F32),
            jax.ShapeDtypeStruct((1, dwidth, n), F32),
        ),
        in_specs=[spec] * 13,
        out_specs=(spec,) * 4,
        scratch_shapes=[
            pltpu.VMEM((heads, toks), F32),
            pltpu.VMEM((n, toks), BF16),
            pltpu.VMEM((toks, toks), F32),
            pltpu.VMEM((chunks, n + ROWS, LANES), F32),
            pltpu.VMEM((toks, LANES), F32),
            pltpu.VMEM((chunks, n, LANES), F32),
            pltpu.VMEM((chunks, n, LANES), F32),
            pltpu.VMEM((chunks, n + ROWS, LANES), F32),
            pltpu.VMEM((chunks, n + ROWS, LANES), F32),
            pltpu.VMEM((dchunks, n, LANES), F32),
            pltpu.VMEM((nb, 2 * steps, dwidth), F32),
            pltpu.VMEM((nb, small_rows, LANES), F32),
            pltpu.VMEM((ROWS, LANES), F32),
            pltpu.VMEM((ROWS, dwidth), F32),
            pltpu.VMEM((ROWS, dwidth), F32),
            pltpu.VMEM((2 * ROWS, dwidth), F32),
            pltpu.VMEM((2 * ROWS, n), F32),
            pltpu.VMEM((ROWS, n), F32),
            dma((chunks,)),
            dma((chunks,)),
            dma((chunks,)),
            dma((chunks,)),
            dma((dchunks, peers)),
            dma((dchunks,)),
            dma((peers,)),
            dma((peers,)),
            dma((peers,)),
            dma((peers,)),
        ],
        compiler_params=pltpu.CompilerParams(
            collective_id=0, has_side_effects=True, vmem_limit_bytes=40 * 1024 * 1024
        ),
    )(x, keys, queries, decay, sv, sk, sq, sd, lp, par, fin, lens.reshape(1, 1), score.reshape(1, 1))


def solution(mesh):
    return jax.shard_map(
        functools.partial(on_device, mesh.shape["seq"], mesh.shape["beam"]),
        mesh=mesh,
        in_specs=(
            P(("groups", "seq"), "beam"),
            P(("groups", "seq"), None),
            P(("groups", "seq"), None),
            P(("groups", "seq"), "beam"),
            P("groups", "beam", "seq"),
            P("groups", "beam", None),
            P("groups", "beam", None),
            P("groups", "beam", "seq"),
            P("groups", "beam"),
            P("groups", "beam"),
            P("groups", "beam"),
            P(("groups", "beam")),
            P(("groups", "beam")),
        ),
        out_specs=(
            P(("groups", "seq"), "beam"),
            P("groups", "beam", "seq"),
            P("groups", "beam"),
            P(("groups", "beam"), "seq", None),
        ),
        check_vma=False,
    )
```

```python
import functools
import math

import jax
import jax.numpy as jnp
from jax import lax
from jax.experimental import pallas as pl
from jax.experimental.pallas import tpu as pltpu
from jax.sharding import PartitionSpec as P

P_SIZE = 64
LANES = 128
PAIR = LANES // P_SIZE
ROWS = 8
HOP = 2
SHARE = 2
START = 2
LOG2E = math.log2(math.e)
MESH = pl.DeviceIdType.MESH
F32 = jnp.float32
BF16 = jnp.bfloat16


def split3(x):
    first = x.astype(BF16)
    rest = x - first.astype(F32)
    second = rest.astype(BF16)
    return first, second, (rest - second.astype(F32)).astype(BF16)


def mm(a, b):
    return jnp.dot(a, b, preferred_element_type=F32)


def mm_first(a, b):
    return lax.dot_general(a, b, (((0,), (0,)), ((), ())), preferred_element_type=F32)


def kernel(
    ns,
    nb,
    x_ref,
    keys_ref,
    queries_ref,
    decay_ref,
    sv_ref,
    sk_ref,
    sq_ref,
    sd_ref,
    lp_ref,
    par_ref,
    fin_ref,
    len_ref,
    score_ref,
    out_ref,
    so_ref,
    rank_ref,
    beam_ref,
    sums_ref,
    cols,
    grown,
    keys_t,
    scores,
    own,
    inner_ref,
    up_recv,
    up_out,
    dn_recv,
    dn_out,
    final,
    vals,
    small,
    pad,
    dec_d,
    dec_add,
    dec_cv,
    dec_k,
    dec_q,
    up_ss,
    up_rs,
    dn_ss,
    dn_rs,
    f_ss,
    f_rs,
    v_ss,
    v_rs,
    m_ss,
    m_rs,
):
    g = lax.axis_index("groups")
    s = lax.axis_index("seq")
    b = lax.axis_index("beam")
    toks, width = x_ref.shape
    n = keys_ref.shape[1]
    chunks = width // LANES
    _, steps, dwidth = sv_ref.shape
    dheads = dwidth // P_SIZE
    dchunks = dwidth // LANES
    last = ns - 1

    barrier = pltpu.get_barrier_semaphore()

    def peer(i):
        return lax.rem(b + i, nb)

    @pl.when(s > 0)
    def _():
        pl.semaphore_signal(barrier, inc=1, device_id=(g, s - 1, b), device_id_type=MESH)

    @pl.when(s < last)
    def _():
        pl.semaphore_signal(barrier, inc=1, device_id=(g, s + 1, b), device_id_type=MESH)

    for i in range(1, nb):
        pl.semaphore_signal(barrier, inc=1, device_id=(g, s, peer(i)), device_id_type=MESH)

    def up_copy(src, k):
        return pltpu.make_async_remote_copy(
            src_ref=src,
            dst_ref=up_recv.at[k],
            send_sem=up_ss.at[k],
            recv_sem=up_rs.at[k],
            device_id=(g, lax.rem(s + 1, ns), b),
            device_id_type=MESH,
        )

    def dn_copy(src, k):
        return pltpu.make_async_remote_copy(
            src_ref=src,
            dst_ref=dn_recv.at[k],
            send_sem=dn_ss.at[k],
            recv_sem=dn_rs.at[k],
            device_id=(g, lax.rem(s + ns - 1, ns), b),
            device_id_type=MESH,
        )

    def f_copy(kk, i):
        return pltpu.make_async_remote_copy(
            src_ref=final.at[kk],
            dst_ref=final.at[kk],
            send_sem=f_ss.at[kk, i - 1],
            recv_sem=f_rs.at[kk],
            device_id=(g, s, peer(i)),
            device_id_type=MESH,
        )

    def v_copy(i):
        return pltpu.make_async_remote_copy(
            src_ref=vals.at[b],
            dst_ref=vals.at[b],
            send_sem=v_ss.at[i - 1],
            recv_sem=v_rs.at[i - 1],
            device_id=(g, s, peer(i)),
            device_id_type=MESH,
        )

    def m_copy(i):
        return pltpu.make_async_remote_copy(
            src_ref=small.at[b],
            dst_ref=small.at[b],
            send_sem=m_ss.at[i - 1],
            recv_sem=m_rs.at[i - 1],
            device_id=(g, s, peer(i)),
            device_id_type=MESH,
        )

    def target(k):
        return (b * chunks + k) // dchunks

    def place(k):
        return lax.rem(b * chunks + k, dchunks)

    row_id = lax.broadcasted_iota(jnp.int32, (toks, toks), 0)
    col_id = lax.broadcasted_iota(jnp.int32, (toks, toks), 1)
    upper = (row_id <= col_id).astype(F32).astype(BF16)
    parts = split3(decay_ref[...] * LOG2E)
    sums_ref[...] = sum(mm(part, upper) for part in reversed(parts))
    keys_t[...] = keys_ref[...].astype(F32).T.astype(BF16)

    left = lax.broadcasted_iota(jnp.int32, (1, LANES), 1) < P_SIZE

    def make_column(head):
        row = sums_ref[pl.ds(head, 1), :]
        column = jnp.broadcast_to(row, (LANES, toks)).T
        cols[head] = column
        return column

    def lanes_of(k):
        return pl.ds(pl.multiple_of(k * LANES, LANES), LANES)

    def make_state(k, carry):
        column = jnp.where(left, make_column(k * PAIR), make_column(k * PAIR + 1))
        end = column[toks - 1 : toks, :]
        scaled = (x_ref[:, lanes_of(k)].astype(F32) * jnp.exp2(end - column)).astype(BF16)
        own[k, 0:n, :] = mm(keys_t[...], scaled)
        grown[k] = jnp.exp2(column)
        own[k, n : n + ROWS, :] = jnp.broadcast_to(jnp.exp2(end), (ROWS, LANES))
        return carry

    def column_of(row):
        row = row.astype(F32)
        pad[...] = jnp.zeros_like(pad)
        for step in range(steps):
            pad[step : step + 1, :] = jnp.broadcast_to(row[:, step : step + 1], (1, LANES))
        return pad[0:steps, :]

    live = 1.0 - column_of(fin_ref[...])
    chance = column_of(lp_ref[...]) * live
    parent_of = column_of(par_ref[...])
    pad[...] = jnp.zeros_like(pad)
    pad[0:steps, 0:dheads] = sd_ref[:, 0, :] * live[:, 0:1] * LOG2E
    spread = (
        lax.broadcasted_iota(jnp.int32, (LANES, dwidth), 0)
        == lax.broadcasted_iota(jnp.int32, (LANES, dwidth), 1) // P_SIZE
    )
    spread = spread.astype(F32).astype(BF16)
    wide = sum(mm(part, spread) for part in reversed(split3(pad[...])))
    vals[b, 0:steps, :] = sv_ref[0].astype(F32) * live[:, 0:1]
    vals[b, steps : 2 * steps, :] = wide[0:steps, :]
    small[b] = jnp.zeros(small.shape[1:], F32)
    small[b, 0:steps, :] = sk_ref[0].astype(F32)
    small[b, steps : 2 * steps, :] = parent_of
    small[b, 2 * steps : 3 * steps, :] = chance
    small[b, 3 * steps : 4 * steps, :] = live
    small[b, 4 * steps : 4 * steps + 1, :] = jnp.full((1, LANES), score_ref[0], F32)
    small[b, 4 * steps + 1 : 4 * steps + 2, :] = jnp.full((1, LANES), len_ref[0], jnp.int32).astype(F32)

    make_state(0, 0)

    met = nb - 1 + jnp.where(s > 0, 1, 0) + jnp.where(s < last, 1, 0)
    pl.semaphore_wait(barrier, met)

    for i in range(1, nb):
        m_copy(i).start()
        v_copy(i).start()

    def first_sends(k):
        @pl.when((s == 0) & (s < last))
        def _():
            up_copy(own.at[k, pl.ds(0, n)], k).start()

        @pl.when((s == last) & (s > target(k)))
        def _():
            dn_copy(own.at[k], k).start()

    first_sends(0)

    def state_and_send(k, carry):
        make_state(k, 0)
        first_sends(k)
        return carry

    lax.fori_loop(1, chunks, state_and_send, 0)

    scores[...] = jnp.where(row_id >= col_id, mm(queries_ref[...], keys_t[...]), 0.0)

    pad[...] = jnp.zeros_like(pad)
    pad[0:steps, :] = live
    dec_d[...] = jnp.zeros_like(dec_d)
    dec_add[...] = jnp.zeros_like(dec_add)
    dec_cv[...] = jnp.zeros_like(dec_cv)
    dec_k[...] = jnp.zeros_like(dec_k)
    dec_q[...] = jnp.zeros_like(dec_q)
    dec_q[0:steps, :] = sq_ref[0].astype(F32)
    own_slot = [jnp.where(b == slot, jnp.ones((1, LANES), F32), 0.0) for slot in range(nb)]

    def pick(weights, ref, row):
        total = None
        for slot in range(nb):
            value = ref[slot, row : row + 1, :]
            weight = weights[slot] if value.shape[1] == LANES else weights[slot][:, 0:1]
            total = weight * value if total is None else total + weight * value
        return total

    def prepare(step):
        chain = own_slot
        decay = jnp.zeros((1, dwidth), F32)
        added = jnp.zeros((1, dwidth), F32)
        query = dec_q[step : step + 1, :]
        for t in range(step, -1, -1):
            value = jnp.exp2(decay) * pick(chain, vals, t)
            key = pick(chain, small, t)
            added = added + jnp.sum(key * query, axis=1, keepdims=True) * value
            decay = decay + pick(chain, vals, steps + t)
            if step == steps - 1:
                high = value.astype(BF16).astype(F32)
                dec_cv[t : t + 1, :] = high
                dec_cv[ROWS + t : ROWS + t + 1, :] = value - high
                dec_k[t : t + 1, :] = key
                dec_k[ROWS + t : ROWS + t + 1, :] = key
            if t > 0:
                parent = pick(chain, small, steps + t)
                chain = [jnp.where(parent == float(slot), 1.0, 0.0) for slot in range(nb)]
        open_now = pad[step : step + 1, 0:1]
        dec_d[step : step + 1, :] = jnp.exp2(decay)
        dec_add[step : step + 1, :] = added * open_now

    def rank_slots():
        score = [small[slot, 4 * steps : 4 * steps + 1, :] for slot in range(nb)]
        length = [small[slot, 4 * steps + 1 : 4 * steps + 2, :] for slot in range(nb)]
        for step in range(steps):
            new_score, new_length, normed = [], [], []
            for slot in range(nb):
                parent = small[slot, steps + step : steps + step + 1, :]
                picked_score, picked_length = score[0], length[0]
                for other in range(1, nb):
                    picked_score = jnp.where(parent == float(other), score[other], picked_score)
                    picked_length = jnp.where(parent == float(other), length[other], picked_length)
                new_score.append(picked_score + small[slot, 2 * steps + step : 2 * steps + step + 1, :])
                new_length.append(picked_length + small[slot, 3 * steps + step : 3 * steps + step + 1, :])
                normed.append(new_score[-1] / jnp.exp(0.6 * jnp.log((5.0 + new_length[-1]) / 6.0)))
            score, length = new_score, new_length
            best = functools.reduce(jnp.maximum, normed)
            mine = sum(own_slot[slot] * normed[slot] for slot in range(nb))
            rank_ref[:, step : step + 1] = (mine - best)[:, 0:1]

    def forward_down(k):
        dn_copy(dn_out.at[k], k).wait_recv()
        shrink = dn_recv[k, n : n + 1, :]
        dn_out[k, 0:n, :] = dn_recv[k, 0:n, :] + shrink * own[k, 0:n, :]
        dn_out[k, n : n + ROWS, :] = dn_recv[k, n : n + ROWS, :] * own[k, n : n + ROWS, :]
        dn_copy(dn_out.at[k], k).start()

    def finish(kk):
        at = lanes_of(kk)
        state = final[kk]
        read = mm(dec_q[...].astype(BF16), state.astype(BF16))
        keep = pad[:, 0:1]
        dec_add[:, at] = keep * (dec_d[:, at] * read) + dec_add[:, at]
        outer = mm_first(dec_cv[:, at].astype(BF16), dec_k[...].astype(BF16))
        rows = pl.ds(pl.multiple_of(kk * LANES, LANES), LANES)
        beam_ref[0, rows, :] = (state * dec_d[steps - 1 : steps, at]).T + outer

    def await_and_finish(kk):
        @pl.when(b != (s * dchunks) // chunks)
        def _():
            f_copy(kk, 1).wait_recv()

        finish(kk)

    up_lag = s * HOP
    dn_lag = (last - s) * HOP
    own_lag = jnp.maximum(jnp.maximum(up_lag, dn_lag), START + steps - SHARE)
    first = lax.rem(s * dchunks, chunks)
    slots = chunks + max(last * HOP, START + steps - SHARE) + SHARE

    def inside(k):
        return (k >= 0) & (k < chunks)

    def make_inner(k):
        values = x_ref[:, lanes_of(k)]
        for i in range(toks // LANES):
            at = slice(i * LANES, (i + 1) * LANES)
            until = (i + 1) * LANES
            made = []
            for j in range(PAIR):
                row = sums_ref[pl.ds(k * PAIR + j, 1), :]
                col = cols[k * PAIR + j, at, :]
                blocks = []
                for other in range(i + 1):
                    to = slice(other * LANES, (other + 1) * LANES)
                    gap = jnp.minimum(col - row[:, to], 0.0)
                    blocks.append((scores[at, to] * jnp.exp2(gap)).astype(BF16))
                weights = blocks[0] if i == 0 else jnp.concatenate(blocks, axis=1)
                made.append(mm(weights, values[0:until, :]))
            inner_ref[k, at, :] = jnp.where(left, made[0], made[1])

    def take_up(k):
        @pl.when(s == 0)
        def _():
            up_out[k] = own[k, 0:n, :]
            out_ref[:, lanes_of(k)] = inner_ref[k].astype(BF16)

        @pl.when(s > 0)
        def _():
            up_copy(up_out.at[k], k).wait_recv()
            up_out[k] = own[k, n : n + 1, :] * up_recv[k] + own[k, 0:n, :]

            @pl.when(s < last)
            def _():
                up_copy(up_out.at[k], k).start()

            carried = mm(queries_ref[...], up_recv[k].astype(BF16)) * grown[k]
            out_ref[:, lanes_of(k)] = (inner_ref[k] + carried).astype(BF16)

    def share_final(k):
        kk = place(k)

        @pl.when(s < last)
        def _():
            dn_copy(dn_out.at[k], k).wait_recv()
            final[kk] = dn_recv[k, n : n + 1, :] * up_out[k] + dn_recv[k, 0:n, :]

        @pl.when(s == last)
        def _():
            final[kk] = up_out[k]

        for i in range(1, nb):
            f_copy(kk, i).start()

    def body(slot, carry):
        for step in range(steps):

            @pl.when(slot == START + step)
            def _():
                if step == 0:
                    for i in range(1, nb):
                        m_copy(i).wait_recv()
                        v_copy(i).wait_recv()
                prepare(step)

        @pl.when(slot < chunks)
        def _():
            make_inner(slot)

        @pl.when(inside(slot - up_lag))
        def _():
            take_up(slot - up_lag)

        down = slot - dn_lag

        @pl.when(inside(down) & (s > target(down)) & (s < last))
        def _():
            forward_down(down)

        at_end = slot - own_lag

        @pl.when(inside(at_end) & (s == target(at_end)))
        def _():
            share_final(at_end)

        kk = slot - own_lag - SHARE - first

        @pl.when((kk >= 0) & (kk < dchunks))
        def _():
            await_and_finish(kk)

        return carry

    lax.fori_loop(0, slots, body, 0)
    rank_slots()
    for step in range(steps):
        so_ref[:, step : step + 1, :] = dec_add[step : step + 1, :].astype(BF16)[None]

    for i in range(1, nb):
        m_copy(i).wait_send()
        v_copy(i).wait_send()

    def drain(k, carry):
        @pl.when(s < last)
        def _():
            up_copy(up_out.at[k], k).wait_send()

        @pl.when(s > target(k))
        def _():
            dn_copy(dn_out.at[k], k).wait_send()

        @pl.when(s == target(k))
        def _():
            for i in range(1, nb):
                f_copy(place(k), i).wait_send()

        return carry

    lax.fori_loop(0, chunks, drain, 0)


def on_device(ns, nb, *args):
    x, keys, queries, decay, sv, sk, sq, sd, lp, par, fin, lens, score = args
    toks, width = x.shape
    n = keys.shape[1]
    heads = decay.shape[1]
    steps, _, dwidth = sv.shape
    chunks, dchunks = width // LANES, dwidth // LANES
    small_rows = -(-(4 * steps + 2) // ROWS) * ROWS
    dma = pltpu.SemaphoreType.DMA
    spec = pl.BlockSpec(memory_space=pltpu.VMEM)
    scalar = pl.BlockSpec(memory_space=pltpu.SMEM)
    peers = max(nb - 1, 1)
    turn = lambda a: jnp.transpose(a, (1, 0, 2))
    prompt, step_out, ranked, states = pl.pallas_call(
        functools.partial(kernel, ns, nb),
        out_shape=(
            jax.ShapeDtypeStruct((toks, width), BF16),
            jax.ShapeDtypeStruct((1, steps, dwidth), BF16),
            jax.ShapeDtypeStruct((1, steps), F32),
            jax.ShapeDtypeStruct((1, dwidth, n), F32),
        ),
        in_specs=[spec] * 11 + [scalar] * 2,
        out_specs=(spec,) * 4,
        scratch_shapes=[
            pltpu.VMEM((heads, toks), F32),
            pltpu.VMEM((heads, toks, LANES), F32),
            pltpu.VMEM((chunks, toks, LANES), F32),
            pltpu.VMEM((n, toks), BF16),
            pltpu.VMEM((toks, toks), F32),
            pltpu.VMEM((chunks, n + ROWS, LANES), F32),
            pltpu.VMEM((chunks, toks, LANES), F32),
            pltpu.VMEM((chunks, n, LANES), F32),
            pltpu.VMEM((chunks, n, LANES), F32),
            pltpu.VMEM((chunks, n + ROWS, LANES), F32),
            pltpu.VMEM((chunks, n + ROWS, LANES), F32),
            pltpu.VMEM((dchunks, n, LANES), F32),
            pltpu.VMEM((nb, 2 * steps, dwidth), F32),
            pltpu.VMEM((nb, small_rows, LANES), F32),
            pltpu.VMEM((ROWS, LANES), F32),
            pltpu.VMEM((ROWS, dwidth), F32),
            pltpu.VMEM((ROWS, dwidth), F32),
            pltpu.VMEM((2 * ROWS, dwidth), F32),
            pltpu.VMEM((2 * ROWS, n), F32),
            pltpu.VMEM((ROWS, n), F32),
            dma((chunks,)),
            dma((chunks,)),
            dma((chunks,)),
            dma((chunks,)),
            dma((dchunks, peers)),
            dma((dchunks,)),
            dma((peers,)),
            dma((peers,)),
            dma((peers,)),
            dma((peers,)),
        ],
        compiler_params=pltpu.CompilerParams(
            collective_id=0, has_side_effects=True, vmem_limit_bytes=40 * 1024 * 1024
        ),
    )(x, keys, queries, decay.T, turn(sv), turn(sk), turn(sq), sd, lp.T, par.T, fin.T, lens, score)
    return prompt, turn(step_out), ranked.T, states


def solution(mesh):
    return jax.shard_map(
        functools.partial(on_device, mesh.shape["seq"], mesh.shape["beam"]),
        mesh=mesh,
        in_specs=(
            P(("groups", "seq"), "beam"),
            P(("groups", "seq"), None),
            P(("groups", "seq"), None),
            P(("groups", "seq"), "beam"),
            P("groups", "beam", "seq"),
            P("groups", "beam", None),
            P("groups", "beam", None),
            P("groups", "beam", "seq"),
            P("groups", "beam"),
            P("groups", "beam"),
            P("groups", "beam"),
            P(("groups", "beam")),
            P(("groups", "beam")),
        ),
        out_specs=(
            P(("groups", "seq"), "beam"),
            P("groups", "beam", "seq"),
            P("groups", "beam"),
            P(("groups", "beam"), "seq", None),
        ),
        check_vma=False,
    )
```

```python
import functools
import math

import jax
import jax.numpy as jnp
from jax import lax
from jax.experimental import pallas as pl
from jax.experimental.pallas import tpu as pltpu
from jax.sharding import PartitionSpec as P

P_SIZE = 64
LANES = 128
PAIR = LANES // P_SIZE
ROWS = 8
HOP = 2
RELAY = 2
SHARE = 4
START = 4
CORES = 2
LOG2E = math.log2(math.e)
MESH = pl.DeviceIdType.MESH
F32 = jnp.float32
BF16 = jnp.bfloat16


def split3(x):
    first = x.astype(BF16)
    rest = x - first.astype(F32)
    second = rest.astype(BF16)
    return first, second, (rest - second.astype(F32)).astype(BF16)


def mm(a, b):
    return jnp.dot(a, b, preferred_element_type=F32)


def mm_first(a, b):
    return lax.dot_general(a, b, (((0,), (0,)), ((), ())), preferred_element_type=F32)


def kernel(
    ns,
    nb,
    x_in,
    keys_in,
    queries_in,
    decay_in,
    sv_in,
    sk_in,
    sq_in,
    sd_in,
    lp_in,
    par_in,
    fin_in,
    len_in,
    score_in,
    out_ref,
    so_ref,
    rank_ref,
    beam_ref,
    x_ref,
    keys_ref,
    queries_ref,
    decay_ref,
    sv_ref,
    sk_ref,
    sq_ref,
    sd_ref,
    lp_ref,
    par_ref,
    fin_ref,
    len_ref,
    score_ref,
    in_sem,
    sums_ref,
    cols,
    grown,
    keys_t,
    scores,
    own,
    inner_ref,
    up_recv,
    up_out,
    dn_recv,
    dn_out,
    final,
    vals,
    small,
    pad,
    dec_d,
    dec_add,
    dec_cv,
    dec_k,
    dec_q,
    up_ss,
    up_rs,
    dn_ss,
    dn_rs,
    f_ss,
    f_rs,
    v_ss,
    v_rs,
    m_ss,
    m_rs,
):
    g = lax.axis_index("groups")
    s = lax.axis_index("seq")
    b = lax.axis_index("beam")
    toks, width = x_ref.shape
    n = keys_ref.shape[1]
    chunks = width // LANES
    _, steps, dwidth = sv_ref.shape
    dheads = dwidth // P_SIZE
    dchunks = dwidth // LANES
    last = ns - 1

    loads = [
        pltpu.make_async_copy(source, here, in_sem.at[i])
        for i, (source, here) in enumerate(
            (
                (decay_in, decay_ref),
                (keys_in, keys_ref),
                (x_in, x_ref),
                (fin_in, fin_ref),
                (sd_in, sd_ref),
                (sv_in, sv_ref),
                (sk_in, sk_ref),
                (lp_in, lp_ref),
                (par_in, par_ref),
                (queries_in, queries_ref),
                (sq_in, sq_ref),
                (len_in, len_ref),
                (score_in, score_ref),
            )
        )
    ]
    for load in loads:
        load.start()

    barrier = pltpu.get_barrier_semaphore()

    def peer(i):
        return lax.rem(b + i, nb)

    @pl.when(s > 0)
    def _():
        pl.semaphore_signal(barrier, inc=1, device_id=(g, s - 1, b), device_id_type=MESH)

    @pl.when(s < last)
    def _():
        pl.semaphore_signal(barrier, inc=1, device_id=(g, s + 1, b), device_id_type=MESH)

    for i in range(1, nb):
        pl.semaphore_signal(barrier, inc=1, device_id=(g, s, peer(i)), device_id_type=MESH)

    def up_copy(src, k):
        return pltpu.make_async_remote_copy(
            src_ref=src,
            dst_ref=up_recv.at[k],
            send_sem=up_ss.at[k],
            recv_sem=up_rs.at[k],
            device_id=(g, lax.rem(s + 1, ns), b),
            device_id_type=MESH,
        )

    def dn_copy(src, k):
        return pltpu.make_async_remote_copy(
            src_ref=src,
            dst_ref=dn_recv.at[k],
            send_sem=dn_ss.at[k],
            recv_sem=dn_rs.at[k],
            device_id=(g, lax.rem(s + ns - 1, ns), b),
            device_id_type=MESH,
        )

    owner = (s * dchunks) // chunks
    mates = nb // CORES
    chip, core = b // CORES, lax.rem(b, CORES)
    other_core = chip * CORES + (CORES - 1 - core)
    is_owner = b == owner
    relays = (core == lax.rem(owner, CORES)) & (b != owner)
    near = relays | (chip == owner // CORES)

    def f_copy(kk, i):
        to = other_core if i == 0 else lax.rem(chip + i, mates) * CORES + core
        return pltpu.make_async_remote_copy(
            src_ref=final.at[kk],
            dst_ref=final.at[kk],
            send_sem=f_ss.at[kk, i],
            recv_sem=f_rs.at[kk],
            device_id=(g, s, to),
            device_id_type=MESH,
        )

    def v_copy(i):
        return pltpu.make_async_remote_copy(
            src_ref=vals.at[b],
            dst_ref=vals.at[b],
            send_sem=v_ss.at[i - 1],
            recv_sem=v_rs.at[i - 1],
            device_id=(g, s, peer(i)),
            device_id_type=MESH,
        )

    def m_copy(i):
        return pltpu.make_async_remote_copy(
            src_ref=small.at[b],
            dst_ref=small.at[b],
            send_sem=m_ss.at[i - 1],
            recv_sem=m_rs.at[i - 1],
            device_id=(g, s, peer(i)),
            device_id_type=MESH,
        )

    def target(k):
        return (b * chunks + k) // dchunks

    def place(k):
        return lax.rem(b * chunks + k, dchunks)

    for load in loads[:3]:
        load.wait()

    row_id = lax.broadcasted_iota(jnp.int32, (toks, toks), 0)
    col_id = lax.broadcasted_iota(jnp.int32, (toks, toks), 1)
    upper = (row_id <= col_id).astype(F32).astype(BF16)
    parts = split3(decay_ref[...] * LOG2E)
    sums_ref[...] = sum(mm(part, upper) for part in reversed(parts))
    keys_t[...] = keys_ref[...].astype(F32).T.astype(BF16)

    left = lax.broadcasted_iota(jnp.int32, (1, LANES), 1) < P_SIZE

    def make_column(head):
        row = sums_ref[pl.ds(head, 1), :]
        column = jnp.broadcast_to(row, (LANES, toks)).T
        cols[head] = column
        return column

    def lanes_of(k):
        return pl.ds(pl.multiple_of(k * LANES, LANES), LANES)

    def make_state(k, carry):
        column = jnp.where(left, make_column(k * PAIR), make_column(k * PAIR + 1))
        end = column[toks - 1 : toks, :]
        scaled = (x_ref[:, lanes_of(k)].astype(F32) * jnp.exp2(end - column)).astype(BF16)
        own[k, 0:n, :] = mm(keys_t[...], scaled)
        grown[k] = jnp.exp2(column)
        own[k, n : n + ROWS, :] = jnp.broadcast_to(jnp.exp2(end), (ROWS, LANES))
        return carry

    make_state(0, 0)

    met = nb - 1 + jnp.where(s > 0, 1, 0) + jnp.where(s < last, 1, 0)
    pl.semaphore_wait(barrier, met)

    def first_sends(k):
        @pl.when((s == 0) & (s < last))
        def _():
            up_copy(own.at[k, pl.ds(0, n)], k).start()

        @pl.when((s == last) & (s > target(k)))
        def _():
            dn_copy(own.at[k], k).start()

    first_sends(0)

    def state_and_send(k, carry):
        make_state(k, 0)
        first_sends(k)
        return carry

    at_edge = (s == 0) | (s == last)

    @pl.when(at_edge)
    def _():
        lax.fori_loop(1, chunks, state_and_send, 0)

    for load in loads[3:]:
        load.wait()

    def column_of(row):
        row = row.astype(F32)
        pad[...] = jnp.zeros_like(pad)
        for step in range(steps):
            pad[step : step + 1, :] = jnp.broadcast_to(row[:, step : step + 1], (1, LANES))
        return pad[0:steps, :]

    live = 1.0 - column_of(fin_ref[...])
    chance = column_of(lp_ref[...]) * live
    parent_of = column_of(par_ref[...])
    pad[...] = jnp.zeros_like(pad)
    pad[0:steps, 0:dheads] = sd_ref[:, 0, :] * live[:, 0:1] * LOG2E
    spread = (
        lax.broadcasted_iota(jnp.int32, (LANES, dwidth), 0)
        == lax.broadcasted_iota(jnp.int32, (LANES, dwidth), 1) // P_SIZE
    )
    spread = spread.astype(F32).astype(BF16)
    wide = sum(mm(part, spread) for part in reversed(split3(pad[...])))
    vals[b, 0:steps, :] = sv_ref[0].astype(F32) * live[:, 0:1]
    vals[b, steps : 2 * steps, :] = wide[0:steps, :]
    small[b] = jnp.zeros(small.shape[1:], F32)
    small[b, 0:steps, :] = sk_ref[0].astype(F32)
    small[b, steps : 2 * steps, :] = parent_of
    small[b, 2 * steps : 3 * steps, :] = chance
    small[b, 3 * steps : 4 * steps, :] = live
    small[b, 4 * steps : 4 * steps + 1, :] = jnp.full((1, LANES), score_ref[0], F32)
    small[b, 4 * steps + 1 : 4 * steps + 2, :] = jnp.full((1, LANES), len_ref[0], jnp.int32).astype(F32)

    for i in range(1, nb):
        m_copy(i).start()
        v_copy(i).start()

    scores[...] = jnp.where(row_id >= col_id, mm(queries_ref[...], keys_t[...]), 0.0)

    pad[...] = jnp.zeros_like(pad)
    pad[0:steps, :] = live
    dec_d[...] = jnp.zeros_like(dec_d)
    dec_add[...] = jnp.zeros_like(dec_add)
    dec_cv[...] = jnp.zeros_like(dec_cv)
    dec_k[...] = jnp.zeros_like(dec_k)
    dec_q[...] = jnp.zeros_like(dec_q)
    dec_q[0:steps, :] = sq_ref[0].astype(F32)
    own_slot = [jnp.where(b == slot, jnp.ones((1, LANES), F32), 0.0) for slot in range(nb)]

    def pick(weights, ref, row):
        total = None
        for slot in range(nb):
            value = ref[slot, row : row + 1, :]
            weight = weights[slot] if value.shape[1] == LANES else weights[slot][:, 0:1]
            total = weight * value if total is None else total + weight * value
        return total

    def prepare(step):
        chain = own_slot
        decay = jnp.zeros((1, dwidth), F32)
        added = jnp.zeros((1, dwidth), F32)
        query = dec_q[step : step + 1, :]
        for t in range(step, -1, -1):
            value = jnp.exp2(decay) * pick(chain, vals, t)
            key = pick(chain, small, t)
            added = added + jnp.sum(key * query, axis=1, keepdims=True) * value
            decay = decay + pick(chain, vals, steps + t)
            if step == steps - 1:
                high = value.astype(BF16).astype(F32)
                dec_cv[t : t + 1, :] = high
                dec_cv[ROWS + t : ROWS + t + 1, :] = value - high
                dec_k[t : t + 1, :] = key
                dec_k[ROWS + t : ROWS + t + 1, :] = key
            if t > 0:
                parent = pick(chain, small, steps + t)
                chain = [jnp.where(parent == float(slot), 1.0, 0.0) for slot in range(nb)]
        open_now = pad[step : step + 1, 0:1]
        dec_d[step : step + 1, :] = jnp.exp2(decay)
        dec_add[step : step + 1, :] = added * open_now

    def rank_slots():
        score = [small[slot, 4 * steps : 4 * steps + 1, :] for slot in range(nb)]
        length = [small[slot, 4 * steps + 1 : 4 * steps + 2, :] for slot in range(nb)]
        for step in range(steps):
            new_score, new_length, normed = [], [], []
            for slot in range(nb):
                parent = small[slot, steps + step : steps + step + 1, :]
                picked_score, picked_length = score[0], length[0]
                for other in range(1, nb):
                    picked_score = jnp.where(parent == float(other), score[other], picked_score)
                    picked_length = jnp.where(parent == float(other), length[other], picked_length)
                new_score.append(picked_score + small[slot, 2 * steps + step : 2 * steps + step + 1, :])
                new_length.append(picked_length + small[slot, 3 * steps + step : 3 * steps + step + 1, :])
                normed.append(new_score[-1] / jnp.exp(0.6 * jnp.log((5.0 + new_length[-1]) / 6.0)))
            score, length = new_score, new_length
            best = functools.reduce(jnp.maximum, normed)
            mine = sum(own_slot[slot] * normed[slot] for slot in range(nb))
            rank_ref[:, step : step + 1] = (mine - best)[:, 0:1]

    def forward_down(k):
        dn_copy(dn_out.at[k], k).wait_recv()
        shrink = dn_recv[k, n : n + 1, :]
        dn_out[k, 0:n, :] = dn_recv[k, 0:n, :] + shrink * own[k, 0:n, :]
        dn_out[k, n : n + ROWS, :] = dn_recv[k, n : n + ROWS, :] * own[k, n : n + ROWS, :]
        dn_copy(dn_out.at[k], k).start()

    def finish(kk):
        at = lanes_of(kk)
        state = final[kk]
        read = mm(dec_q[...].astype(BF16), state.astype(BF16))
        keep = pad[:, 0:1]
        dec_add[:, at] = keep * (dec_d[:, at] * read) + dec_add[:, at]
        outer = mm_first(dec_cv[:, at].astype(BF16), dec_k[...].astype(BF16))
        rows = pl.ds(pl.multiple_of(kk * LANES, LANES), LANES)
        beam_ref[0, rows, :] = (state * dec_d[steps - 1 : steps, at]).T + outer

    def await_and_finish(kk):
        @pl.when(b != owner)
        def _():
            f_copy(kk, 0).wait_recv()

        @pl.when(relays)
        def _():
            f_copy(kk, 0).start()

        finish(kk)

    up_lag = s * HOP
    dn_lag = (last - s) * HOP
    own_lag = jnp.maximum(jnp.maximum(up_lag, dn_lag), START + steps)
    first = lax.rem(s * dchunks, chunks)
    slots = chunks + max(last * HOP, START + steps) + SHARE

    def inside(k):
        return (k >= 0) & (k < chunks)

    def make_inner(k):
        values = x_ref[:, lanes_of(k)]
        for i in range(toks // LANES):
            at = slice(i * LANES, (i + 1) * LANES)
            until = (i + 1) * LANES
            made = []
            for j in range(PAIR):
                row = sums_ref[pl.ds(k * PAIR + j, 1), :]
                col = cols[k * PAIR + j, at, :]
                blocks = []
                for other in range(i + 1):
                    to = slice(other * LANES, (other + 1) * LANES)
                    gap = jnp.minimum(col - row[:, to], 0.0)
                    blocks.append((scores[at, to] * jnp.exp2(gap)).astype(BF16))
                weights = blocks[0] if i == 0 else jnp.concatenate(blocks, axis=1)
                made.append(mm(weights, values[0:until, :]))
            inner_ref[k, at, :] = jnp.where(left, made[0], made[1])

    def take_up(k):
        @pl.when(s == 0)
        def _():
            up_out[k] = own[k, 0:n, :]
            out_ref[:, lanes_of(k)] = inner_ref[k].astype(BF16)

        @pl.when(s > 0)
        def _():
            up_copy(up_out.at[k], k).wait_recv()
            up_out[k] = own[k, n : n + 1, :] * up_recv[k] + own[k, 0:n, :]

            @pl.when(s < last)
            def _():
                up_copy(up_out.at[k], k).start()

            carried = mm(queries_ref[...], up_recv[k].astype(BF16)) * grown[k]
            out_ref[:, lanes_of(k)] = (inner_ref[k] + carried).astype(BF16)

    def share_final(k):
        kk = place(k)

        @pl.when(s < last)
        def _():
            dn_copy(dn_out.at[k], k).wait_recv()
            final[kk] = dn_recv[k, n : n + 1, :] * up_out[k] + dn_recv[k, 0:n, :]

        @pl.when(s == last)
        def _():
            final[kk] = up_out[k]

        for i in range(mates):
            f_copy(kk, i).start()

    def body(slot, carry):
        for step in range(steps):

            @pl.when(slot == START + step)
            def _():
                if step == 0:
                    for i in range(1, nb):
                        m_copy(i).wait_recv()
                        v_copy(i).wait_recv()
                prepare(step)

        @pl.when((slot > 0) & (slot < chunks) & (s > 0) & (s < last))
        def _():
            make_state(slot, 0)

        @pl.when(slot < chunks)
        def _():
            make_inner(slot)

        @pl.when(inside(slot - up_lag))
        def _():
            take_up(slot - up_lag)

        down = slot - dn_lag

        @pl.when(inside(down) & (s > target(down)) & (s < last))
        def _():
            forward_down(down)

        at_end = slot - own_lag

        @pl.when(inside(at_end) & (s == target(at_end)))
        def _():
            share_final(at_end)

        kk = slot - own_lag - first - jnp.where(is_owner, 0, jnp.where(near, RELAY, SHARE))

        @pl.when((kk >= 0) & (kk < dchunks))
        def _():
            await_and_finish(kk)

        return carry

    lax.fori_loop(0, slots, body, 0)
    rank_slots()
    for step in range(steps):
        so_ref[:, step : step + 1, :] = dec_add[step : step + 1, :].astype(BF16)[None]

    for i in range(1, nb):
        m_copy(i).wait_send()
        v_copy(i).wait_send()

    def drain(k, carry):
        @pl.when(s < last)
        def _():
            up_copy(up_out.at[k], k).wait_send()

        @pl.when(s > target(k))
        def _():
            dn_copy(dn_out.at[k], k).wait_send()

        @pl.when(s == target(k))
        def _():
            for i in range(mates):
                f_copy(place(k), i).wait_send()

        return carry

    lax.fori_loop(0, chunks, drain, 0)

    @pl.when(relays)
    def _():
        def drain_relay(kk, carry):
            f_copy(kk, 0).wait_send()
            return carry

        lax.fori_loop(0, dchunks, drain_relay, 0)


def on_device(ns, nb, *args):
    x, keys, queries, decay, sv, sk, sq, sd, lp, par, fin, lens, score = args
    toks, width = x.shape
    n = keys.shape[1]
    heads = decay.shape[1]
    steps, _, dwidth = sv.shape
    chunks, dchunks = width // LANES, dwidth // LANES
    small_rows = -(-(4 * steps + 2) // ROWS) * ROWS
    dma = pltpu.SemaphoreType.DMA
    spec = pl.BlockSpec(memory_space=pltpu.VMEM)
    outside = pl.BlockSpec(memory_space=pl.ANY)
    peers = max(nb - 1, 1)
    turn = lambda a: jnp.transpose(a, (1, 0, 2))
    inputs = (x, keys, queries, decay.T, turn(sv), turn(sk), turn(sq), sd, lp.T, par.T, fin.T, lens, score)
    prompt, step_out, ranked, states = pl.pallas_call(
        functools.partial(kernel, ns, nb),
        out_shape=(
            jax.ShapeDtypeStruct((toks, width), BF16),
            jax.ShapeDtypeStruct((1, steps, dwidth), BF16),
            jax.ShapeDtypeStruct((1, steps), F32),
            jax.ShapeDtypeStruct((1, dwidth, n), F32),
        ),
        in_specs=[outside] * 13,
        out_specs=(spec,) * 4,
        scratch_shapes=[
            *[pltpu.VMEM(a.shape, a.dtype) for a in inputs[:11]],
            *[pltpu.SMEM(a.shape, a.dtype) for a in inputs[11:]],
            dma((len(inputs),)),
            pltpu.VMEM((heads, toks), F32),
            pltpu.VMEM((heads, toks, LANES), F32),
            pltpu.VMEM((chunks, toks, LANES), F32),
            pltpu.VMEM((n, toks), BF16),
            pltpu.VMEM((toks, toks), F32),
            pltpu.VMEM((chunks, n + ROWS, LANES), F32),
            pltpu.VMEM((chunks, toks, LANES), F32),
            pltpu.VMEM((chunks, n, LANES), F32),
            pltpu.VMEM((chunks, n, LANES), F32),
            pltpu.VMEM((chunks, n + ROWS, LANES), F32),
            pltpu.VMEM((chunks, n + ROWS, LANES), F32),
            pltpu.VMEM((dchunks, n, LANES), F32),
            pltpu.VMEM((nb, 2 * steps, dwidth), F32),
            pltpu.VMEM((nb, small_rows, LANES), F32),
            pltpu.VMEM((ROWS, LANES), F32),
            pltpu.VMEM((ROWS, dwidth), F32),
            pltpu.VMEM((ROWS, dwidth), F32),
            pltpu.VMEM((2 * ROWS, dwidth), F32),
            pltpu.VMEM((2 * ROWS, n), F32),
            pltpu.VMEM((ROWS, n), F32),
            dma((chunks,)),
            dma((chunks,)),
            dma((chunks,)),
            dma((chunks,)),
            dma((dchunks, nb // CORES)),
            dma((dchunks,)),
            dma((peers,)),
            dma((peers,)),
            dma((peers,)),
            dma((peers,)),
        ],
        compiler_params=pltpu.CompilerParams(
            collective_id=0, has_side_effects=True, vmem_limit_bytes=60 * 1024 * 1024
        ),
    )(*inputs)
    return prompt, turn(step_out), ranked.T, states


def solution(mesh):
    return jax.shard_map(
        functools.partial(on_device, mesh.shape["seq"], mesh.shape["beam"]),
        mesh=mesh,
        in_specs=(
            P(("groups", "seq"), "beam"),
            P(("groups", "seq"), None),
            P(("groups", "seq"), None),
            P(("groups", "seq"), "beam"),
            P("groups", "beam", "seq"),
            P("groups", "beam", None),
            P("groups", "beam", None),
            P("groups", "beam", "seq"),
            P("groups", "beam"),
            P("groups", "beam"),
            P("groups", "beam"),
            P(("groups", "beam")),
            P(("groups", "beam")),
        ),
        out_specs=(
            P(("groups", "seq"), "beam"),
            P("groups", "beam", "seq"),
            P("groups", "beam"),
            P(("groups", "beam"), "seq", None),
        ),
        check_vma=False,
    )
```

```python
import functools
import math

import jax
import jax.numpy as jnp
from jax import lax
from jax.experimental import pallas as pl
from jax.experimental.pallas import tpu as pltpu
from jax.sharding import PartitionSpec as P

P_SIZE = 64
LANES = 128
PAIR = LANES // P_SIZE
ROWS = 8
HOP = 3
RELAY = 3
SHARE = 6
START = 4
CORES = 2
LOG2E = math.log2(math.e)
MESH = pl.DeviceIdType.MESH
F32 = jnp.float32
BF16 = jnp.bfloat16


def split3(x):
    first = x.astype(BF16)
    rest = x - first.astype(F32)
    second = rest.astype(BF16)
    return first, second, (rest - second.astype(F32)).astype(BF16)


def mm(a, b):
    return jnp.dot(a, b, preferred_element_type=F32)


def mm_first(a, b):
    return lax.dot_general(a, b, (((0,), (0,)), ((), ())), preferred_element_type=F32)


def kernel(
    ns,
    nb,
    x_in,
    keys_in,
    queries_in,
    decay_in,
    sv_in,
    sk_in,
    sq_in,
    sd_in,
    lp_in,
    par_in,
    fin_in,
    len_in,
    score_in,
    out_ref,
    so_ref,
    rank_ref,
    beam_ref,
    x_ref,
    keys_ref,
    queries_ref,
    decay_ref,
    sv_ref,
    sk_ref,
    sq_ref,
    sd_ref,
    lp_ref,
    par_ref,
    fin_ref,
    len_ref,
    score_ref,
    in_sem,
    sums_ref,
    cols,
    grown,
    keys_t,
    scores,
    own,
    inner_ref,
    up_recv,
    up_out,
    dn_recv,
    dn_out,
    final,
    vals,
    small,
    pad,
    dec_d,
    dec_add,
    dec_cv,
    dec_k,
    dec_q,
    up_ss,
    up_rs,
    dn_ss,
    dn_rs,
    f_ss,
    f_rs,
    v_ss,
    v_rs,
    m_ss,
    m_rs,
    beam_out,
    out_sem,
    beam_sem,
):
    g = lax.axis_index("groups")
    s = lax.axis_index("seq")
    b = lax.axis_index("beam")
    toks, width = x_ref.shape
    n = keys_ref.shape[1]
    chunks = width // LANES
    _, steps, dwidth = sv_ref.shape
    dheads = dwidth // P_SIZE
    dchunks = dwidth // LANES
    last = ns - 1

    loads = [
        pltpu.make_async_copy(source, here, in_sem.at[i])
        for i, (source, here) in enumerate(
            (
                (decay_in, decay_ref),
                (keys_in, keys_ref),
                (x_in, x_ref),
                (fin_in, fin_ref),
                (sd_in, sd_ref),
                (sv_in, sv_ref),
                (sk_in, sk_ref),
                (lp_in, lp_ref),
                (par_in, par_ref),
                (queries_in, queries_ref),
                (sq_in, sq_ref),
                (len_in, len_ref),
                (score_in, score_ref),
            )
        )
    ]
    for load in loads:
        load.start()

    barrier = pltpu.get_barrier_semaphore()

    def peer(i):
        return lax.rem(b + i, nb)

    @pl.when(s > 0)
    def _():
        pl.semaphore_signal(barrier, inc=1, device_id=(g, s - 1, b), device_id_type=MESH)

    @pl.when(s < last)
    def _():
        pl.semaphore_signal(barrier, inc=1, device_id=(g, s + 1, b), device_id_type=MESH)

    for i in range(1, nb):
        pl.semaphore_signal(barrier, inc=1, device_id=(g, s, peer(i)), device_id_type=MESH)

    def lanes_of(k):
        return pl.ds(pl.multiple_of(k * LANES, LANES), LANES)

    def up_copy(src, k):
        return pltpu.make_async_remote_copy(
            src_ref=src,
            dst_ref=up_recv.at[k],
            send_sem=up_ss.at[k],
            recv_sem=up_rs.at[k],
            device_id=(g, lax.rem(s + 1, ns), b),
            device_id_type=MESH,
        )

    def dn_copy(src, k):
        return pltpu.make_async_remote_copy(
            src_ref=src,
            dst_ref=dn_recv.at[k],
            send_sem=dn_ss.at[k],
            recv_sem=dn_rs.at[k],
            device_id=(g, lax.rem(s + ns - 1, ns), b),
            device_id_type=MESH,
        )

    owner = (s * dchunks) // chunks
    mates = nb // CORES
    chip, core = b // CORES, lax.rem(b, CORES)
    other_core = chip * CORES + (CORES - 1 - core)
    is_owner = b == owner
    relays = (core == lax.rem(owner, CORES)) & (b != owner)
    near = relays | (chip == owner // CORES)

    def f_copy(kk, i):
        to = other_core if i == 0 else lax.rem(chip + i, mates) * CORES + core
        return pltpu.make_async_remote_copy(
            src_ref=final.at[kk],
            dst_ref=final.at[kk],
            send_sem=f_ss.at[kk, i],
            recv_sem=f_rs.at[kk],
            device_id=(g, s, to),
            device_id_type=MESH,
        )

    def v_copy(i):
        return pltpu.make_async_remote_copy(
            src_ref=vals.at[b],
            dst_ref=vals.at[b],
            send_sem=v_ss.at[i - 1],
            recv_sem=v_rs.at[i - 1],
            device_id=(g, s, peer(i)),
            device_id_type=MESH,
        )

    def m_copy(i):
        return pltpu.make_async_remote_copy(
            src_ref=small.at[b],
            dst_ref=small.at[b],
            send_sem=m_ss.at[i - 1],
            recv_sem=m_rs.at[i - 1],
            device_id=(g, s, peer(i)),
            device_id_type=MESH,
        )

    def out_copy(k):
        return pltpu.make_async_copy(inner_ref.at[k], out_ref.at[:, lanes_of(k)], out_sem.at[k])

    def beam_copy(kk):
        rows = pl.ds(pl.multiple_of(kk * LANES, LANES), LANES)
        return pltpu.make_async_copy(beam_out.at[kk], beam_ref.at[0, rows], beam_sem.at[kk])

    def target(k):
        return (b * chunks + k) // dchunks

    def place(k):
        return lax.rem(b * chunks + k, dchunks)

    for load in loads[:3]:
        load.wait()

    row_id = lax.broadcasted_iota(jnp.int32, (toks, toks), 0)
    col_id = lax.broadcasted_iota(jnp.int32, (toks, toks), 1)
    upper = (row_id <= col_id).astype(F32).astype(BF16)
    parts = split3(decay_ref[...] * LOG2E)
    sums_ref[...] = sum(mm(part, upper) for part in reversed(parts))
    keys_t[...] = keys_ref[...].astype(F32).T.astype(BF16)

    left = lax.broadcasted_iota(jnp.int32, (1, LANES), 1) < P_SIZE

    def make_column(head):
        row = sums_ref[pl.ds(head, 1), :]
        column = jnp.broadcast_to(row, (LANES, toks)).T
        cols[head] = column
        return column

    def make_state(k, carry):
        column = jnp.where(left, make_column(k * PAIR), make_column(k * PAIR + 1))
        end = column[toks - 1 : toks, :]
        scaled = (x_ref[:, lanes_of(k)].astype(F32) * jnp.exp2(end - column)).astype(BF16)
        own[k, 0:n, :] = mm(keys_t[...], scaled)
        grown[k] = jnp.exp2(column)
        own[k, n : n + ROWS, :] = jnp.broadcast_to(jnp.exp2(end), (ROWS, LANES))
        return carry

    make_state(0, 0)

    met = nb - 1 + jnp.where(s > 0, 1, 0) + jnp.where(s < last, 1, 0)
    pl.semaphore_wait(barrier, met)

    def first_sends(k):
        @pl.when((s == 0) & (s < last))
        def _():
            up_copy(own.at[k, pl.ds(0, n)], k).start()

        @pl.when((s == last) & (s > target(k)))
        def _():
            dn_copy(own.at[k], k).start()

    first_sends(0)

    def state_and_send(k, carry):
        make_state(k, 0)
        first_sends(k)
        return carry

    at_edge = (s == 0) | (s == last)

    @pl.when(at_edge)
    def _():
        lax.fori_loop(1, chunks, state_and_send, 0)

    for load in loads[3:]:
        load.wait()

    def column_of(row):
        row = row.astype(F32)
        pad[...] = jnp.zeros_like(pad)
        for step in range(steps):
            pad[step : step + 1, :] = jnp.broadcast_to(row[:, step : step + 1], (1, LANES))
        return pad[0:steps, :]

    live = 1.0 - column_of(fin_ref[...])
    chance = column_of(lp_ref[...]) * live
    parent_of = column_of(par_ref[...])
    pad[...] = jnp.zeros_like(pad)
    pad[0:steps, 0:dheads] = sd_ref[:, 0, :] * live[:, 0:1] * LOG2E
    spread = (
        lax.broadcasted_iota(jnp.int32, (LANES, dwidth), 0)
        == lax.broadcasted_iota(jnp.int32, (LANES, dwidth), 1) // P_SIZE
    )
    spread = spread.astype(F32).astype(BF16)
    wide = sum(mm(part, spread) for part in reversed(split3(pad[...])))
    vals[b, 0:steps, :] = sv_ref[0].astype(F32) * live[:, 0:1]
    vals[b, steps : 2 * steps, :] = wide[0:steps, :]
    small[b] = jnp.zeros(small.shape[1:], F32)
    small[b, 0:steps, :] = sk_ref[0].astype(F32)
    small[b, steps : 2 * steps, :] = parent_of
    small[b, 2 * steps : 3 * steps, :] = chance
    small[b, 3 * steps : 4 * steps, :] = live
    small[b, 4 * steps : 4 * steps + 1, :] = jnp.full((1, LANES), score_ref[0], F32)
    small[b, 4 * steps + 1 : 4 * steps + 2, :] = jnp.full((1, LANES), len_ref[0], jnp.int32).astype(F32)

    for i in range(1, nb):
        m_copy(i).start()
        v_copy(i).start()

    scores[...] = jnp.where(row_id >= col_id, mm(queries_ref[...], keys_t[...]), 0.0)

    pad[...] = jnp.zeros_like(pad)
    pad[0:steps, :] = live
    dec_d[...] = jnp.zeros_like(dec_d)
    dec_add[...] = jnp.zeros_like(dec_add)
    dec_cv[...] = jnp.zeros_like(dec_cv)
    dec_k[...] = jnp.zeros_like(dec_k)
    dec_q[...] = jnp.zeros_like(dec_q)
    dec_q[0:steps, :] = sq_ref[0].astype(F32)
    own_slot = [jnp.where(b == slot, jnp.ones((1, LANES), F32), 0.0) for slot in range(nb)]

    def pick(weights, ref, row):
        total = None
        for slot in range(nb):
            value = ref[slot, row : row + 1, :]
            weight = weights[slot] if value.shape[1] == LANES else weights[slot][:, 0:1]
            total = weight * value if total is None else total + weight * value
        return total

    def prepare(step):
        chain = own_slot
        decay = jnp.zeros((1, dwidth), F32)
        added = jnp.zeros((1, dwidth), F32)
        query = dec_q[step : step + 1, :]
        for t in range(step, -1, -1):
            value = jnp.exp2(decay) * pick(chain, vals, t)
            key = pick(chain, small, t)
            added = added + jnp.sum(key * query, axis=1, keepdims=True) * value
            decay = decay + pick(chain, vals, steps + t)
            if step == steps - 1:
                high = value.astype(BF16).astype(F32)
                dec_cv[t : t + 1, :] = high
                dec_cv[ROWS + t : ROWS + t + 1, :] = value - high
                dec_k[t : t + 1, :] = key
                dec_k[ROWS + t : ROWS + t + 1, :] = key
            if t > 0:
                parent = pick(chain, small, steps + t)
                chain = [jnp.where(parent == float(slot), 1.0, 0.0) for slot in range(nb)]
        open_now = pad[step : step + 1, 0:1]
        dec_d[step : step + 1, :] = jnp.exp2(decay)
        dec_add[step : step + 1, :] = added * open_now

    def rank_slots():
        score = [small[slot, 4 * steps : 4 * steps + 1, :] for slot in range(nb)]
        length = [small[slot, 4 * steps + 1 : 4 * steps + 2, :] for slot in range(nb)]
        for step in range(steps):
            new_score, new_length, normed = [], [], []
            for slot in range(nb):
                parent = small[slot, steps + step : steps + step + 1, :]
                picked_score, picked_length = score[0], length[0]
                for other in range(1, nb):
                    picked_score = jnp.where(parent == float(other), score[other], picked_score)
                    picked_length = jnp.where(parent == float(other), length[other], picked_length)
                new_score.append(picked_score + small[slot, 2 * steps + step : 2 * steps + step + 1, :])
                new_length.append(picked_length + small[slot, 3 * steps + step : 3 * steps + step + 1, :])
                normed.append(new_score[-1] / jnp.exp(0.6 * jnp.log((5.0 + new_length[-1]) / 6.0)))
            score, length = new_score, new_length
            best = functools.reduce(jnp.maximum, normed)
            mine = sum(own_slot[slot] * normed[slot] for slot in range(nb))
            rank_ref[:, step : step + 1] = (mine - best)[:, 0:1]

    def forward_down(k):
        dn_copy(dn_out.at[k], k).wait_recv()
        shrink = dn_recv[k, n : n + 1, :]
        dn_out[k, 0:n, :] = dn_recv[k, 0:n, :] + shrink * own[k, 0:n, :]
        dn_out[k, n : n + ROWS, :] = dn_recv[k, n : n + ROWS, :] * own[k, n : n + ROWS, :]
        dn_copy(dn_out.at[k], k).start()

    def finish(kk):
        at = lanes_of(kk)
        state = final[kk]
        read = mm(dec_q[...].astype(BF16), state.astype(BF16))
        keep = pad[:, 0:1]
        dec_add[:, at] = keep * (dec_d[:, at] * read) + dec_add[:, at]
        outer = mm_first(dec_cv[:, at].astype(BF16), dec_k[...].astype(BF16))
        beam_out[kk] = (state * dec_d[steps - 1 : steps, at]).T + outer
        beam_copy(kk).start()

    def await_and_finish(kk):
        @pl.when(b != owner)
        def _():
            f_copy(kk, 0).wait_recv()

        @pl.when(relays)
        def _():
            f_copy(kk, 0).start()

        finish(kk)

    up_lag = s * HOP
    dn_lag = (last - s) * HOP
    own_lag = jnp.maximum(jnp.maximum(up_lag, dn_lag), START + steps)
    first = lax.rem(s * dchunks, chunks)
    slots = chunks + max(last * HOP, START + steps) + SHARE

    def inside(k):
        return (k >= 0) & (k < chunks)

    def make_inner(k):
        values = x_ref[:, lanes_of(k)]
        for i in range(toks // LANES):
            at = slice(i * LANES, (i + 1) * LANES)
            until = (i + 1) * LANES
            made = []
            for j in range(PAIR):
                row = sums_ref[pl.ds(k * PAIR + j, 1), :]
                col = cols[k * PAIR + j, at, :]
                blocks = []
                for other in range(i + 1):
                    to = slice(other * LANES, (other + 1) * LANES)
                    gap = jnp.minimum(col - row[:, to], 0.0)
                    blocks.append((scores[at, to] * jnp.exp2(gap)).astype(BF16))
                weights = blocks[0] if i == 0 else jnp.concatenate(blocks, axis=1)
                made.append(mm(weights, values[0:until, :]))
            inner_ref[k, at, :] = jnp.where(left, made[0], made[1])

    def take_up(k):
        @pl.when(s == 0)
        def _():
            up_out[k] = own[k, 0:n, :]
            out_copy(k).start()

        @pl.when(s > 0)
        def _():
            up_copy(up_out.at[k], k).wait_recv()
            up_out[k] = own[k, n : n + 1, :] * up_recv[k] + own[k, 0:n, :]

            @pl.when(s < last)
            def _():
                up_copy(up_out.at[k], k).start()

            carried = mm(queries_ref[...], up_recv[k].astype(BF16)) * grown[k]
            inner_ref[k] = inner_ref[k] + carried
            out_copy(k).start()

    def share_final(k):
        kk = place(k)

        @pl.when(s < last)
        def _():
            dn_copy(dn_out.at[k], k).wait_recv()
            final[kk] = dn_recv[k, n : n + 1, :] * up_out[k] + dn_recv[k, 0:n, :]

        @pl.when(s == last)
        def _():
            final[kk] = up_out[k]

        for i in range(mates):
            f_copy(kk, i).start()

    def body(slot, carry):
        for step in range(steps):

            @pl.when(slot == START + step)
            def _():
                if step == 0:
                    for i in range(1, nb):
                        m_copy(i).wait_recv()
                        v_copy(i).wait_recv()
                prepare(step)

        @pl.when((slot > 0) & (slot < chunks) & (s > 0) & (s < last))
        def _():
            make_state(slot, 0)

        @pl.when(slot < chunks)
        def _():
            make_inner(slot)

        down = slot - dn_lag
        goes_down = inside(down) & (s > target(down)) & (s < last)

        @pl.when(goes_down & (2 * s >= ns))
        def _():
            forward_down(down)

        @pl.when(inside(slot - up_lag))
        def _():
            take_up(slot - up_lag)

        @pl.when(goes_down & (2 * s < ns))
        def _():
            forward_down(down)

        at_end = slot - own_lag

        @pl.when(inside(at_end) & (s == target(at_end)))
        def _():
            share_final(at_end)

        kk = slot - own_lag - first - jnp.where(is_owner, 0, jnp.where(near, RELAY, SHARE))

        @pl.when((kk >= 0) & (kk < dchunks))
        def _():
            await_and_finish(kk)

        return carry

    lax.fori_loop(0, slots, body, 0)
    rank_slots()
    for step in range(steps):
        so_ref[:, step : step + 1, :] = dec_add[step : step + 1, :].astype(BF16)[None]

    for i in range(1, nb):
        m_copy(i).wait_send()
        v_copy(i).wait_send()

    def drain(k, carry):
        @pl.when(s < last)
        def _():
            up_copy(up_out.at[k], k).wait_send()

        @pl.when(s > target(k))
        def _():
            dn_copy(dn_out.at[k], k).wait_send()

        @pl.when(s == target(k))
        def _():
            for i in range(mates):
                f_copy(place(k), i).wait_send()

        return carry

    lax.fori_loop(0, chunks, drain, 0)

    def drain_results(k, carry):
        out_copy(k).wait()
        return carry

    lax.fori_loop(0, chunks, drain_results, 0)

    def drain_states(kk, carry):
        beam_copy(kk).wait()
        return carry

    lax.fori_loop(0, dchunks, drain_states, 0)

    @pl.when(relays)
    def _():
        def drain_relay(kk, carry):
            f_copy(kk, 0).wait_send()
            return carry

        lax.fori_loop(0, dchunks, drain_relay, 0)


def on_device(ns, nb, *args):
    x, keys, queries, decay, sv, sk, sq, sd, lp, par, fin, lens, score = args
    toks, width = x.shape
    n = keys.shape[1]
    heads = decay.shape[1]
    steps, _, dwidth = sv.shape
    chunks, dchunks = width // LANES, dwidth // LANES
    small_rows = -(-(4 * steps + 2) // ROWS) * ROWS
    dma = pltpu.SemaphoreType.DMA
    spec = pl.BlockSpec(memory_space=pltpu.VMEM)
    outside = pl.BlockSpec(memory_space=pl.ANY)
    peers = max(nb - 1, 1)
    turn = lambda a: jnp.transpose(a, (1, 0, 2))
    inputs = (x, keys, queries, decay.T, turn(sv), turn(sk), turn(sq), sd, lp.T, par.T, fin.T, lens, score)
    prompt, step_out, ranked, states = pl.pallas_call(
        functools.partial(kernel, ns, nb),
        out_shape=(
            jax.ShapeDtypeStruct((toks, width), F32),
            jax.ShapeDtypeStruct((1, steps, dwidth), BF16),
            jax.ShapeDtypeStruct((1, steps), F32),
            jax.ShapeDtypeStruct((1, dwidth, n), F32),
        ),
        in_specs=[outside] * 13,
        out_specs=(outside, spec, spec, outside),
        scratch_shapes=[
            *[pltpu.VMEM(a.shape, a.dtype) for a in inputs[:11]],
            *[pltpu.SMEM(a.shape, a.dtype) for a in inputs[11:]],
            dma((len(inputs),)),
            pltpu.VMEM((heads, toks), F32),
            pltpu.VMEM((heads, toks, LANES), F32),
            pltpu.VMEM((chunks, toks, LANES), F32),
            pltpu.VMEM((n, toks), BF16),
            pltpu.VMEM((toks, toks), F32),
            pltpu.VMEM((chunks, n + ROWS, LANES), F32),
            pltpu.VMEM((chunks, toks, LANES), F32),
            pltpu.VMEM((chunks, n, LANES), F32),
            pltpu.VMEM((chunks, n, LANES), F32),
            pltpu.VMEM((chunks, n + ROWS, LANES), F32),
            pltpu.VMEM((chunks, n + ROWS, LANES), F32),
            pltpu.VMEM((dchunks, n, LANES), F32),
            pltpu.VMEM((nb, 2 * steps, dwidth), F32),
            pltpu.VMEM((nb, small_rows, LANES), F32),
            pltpu.VMEM((ROWS, LANES), F32),
            pltpu.VMEM((ROWS, dwidth), F32),
            pltpu.VMEM((ROWS, dwidth), F32),
            pltpu.VMEM((2 * ROWS, dwidth), F32),
            pltpu.VMEM((2 * ROWS, n), F32),
            pltpu.VMEM((ROWS, n), F32),
            dma((chunks,)),
            dma((chunks,)),
            dma((chunks,)),
            dma((chunks,)),
            dma((dchunks, nb // CORES)),
            dma((dchunks,)),
            dma((peers,)),
            dma((peers,)),
            dma((peers,)),
            dma((peers,)),
            pltpu.VMEM((dchunks, LANES, n), F32),
            dma((chunks,)),
            dma((dchunks,)),
        ],
        compiler_params=pltpu.CompilerParams(
            collective_id=0, has_side_effects=True, vmem_limit_bytes=60 * 1024 * 1024
        ),
    )(*inputs)
    return prompt.astype(BF16), turn(step_out), ranked.T, states


def solution(mesh):
    return jax.shard_map(
        functools.partial(on_device, mesh.shape["seq"], mesh.shape["beam"]),
        mesh=mesh,
        in_specs=(
            P(("groups", "seq"), "beam"),
            P(("groups", "seq"), None),
            P(("groups", "seq"), None),
            P(("groups", "seq"), "beam"),
            P("groups", "beam", "seq"),
            P("groups", "beam", None),
            P("groups", "beam", None),
            P("groups", "beam", "seq"),
            P("groups", "beam"),
            P("groups", "beam"),
            P("groups", "beam"),
            P(("groups", "beam")),
            P(("groups", "beam")),
        ),
        out_specs=(
            P(("groups", "seq"), "beam"),
            P("groups", "beam", "seq"),
            P("groups", "beam"),
            P(("groups", "beam"), "seq", None),
        ),
        check_vma=False,
    )
```

```python
import functools
import math

import jax
import jax.numpy as jnp
from jax import lax
from jax.experimental import pallas as pl
from jax.experimental.pallas import tpu as pltpu
from jax.sharding import PartitionSpec as P

P_SIZE = 64
LANES = 128
PAIR = LANES // P_SIZE
ROWS = 8
HOP = 3
RELAY = 3
SHARE = 6
START = 4
CORES = 2
PIECES = 2
LOG2E = math.log2(math.e)
MESH = pl.DeviceIdType.MESH
F32 = jnp.float32
BF16 = jnp.bfloat16


def split3(x):
    first = x.astype(BF16)
    rest = x - first.astype(F32)
    second = rest.astype(BF16)
    return first, second, (rest - second.astype(F32)).astype(BF16)


def mm(a, b):
    return jnp.dot(a, b, preferred_element_type=F32)


def mm_first(a, b):
    return lax.dot_general(a, b, (((0,), (0,)), ((), ())), preferred_element_type=F32)


def kernel(
    ns,
    nb,
    x_in,
    keys_in,
    queries_in,
    decay_in,
    sv_in,
    sk_in,
    sq_in,
    sd_in,
    lp_in,
    par_in,
    fin_in,
    len_in,
    score_in,
    out_ref,
    so_ref,
    rank_ref,
    beam_ref,
    x_ref,
    keys_ref,
    queries_ref,
    decay_ref,
    sv_ref,
    sk_ref,
    sq_ref,
    sd_ref,
    lp_ref,
    par_ref,
    fin_ref,
    len_ref,
    score_ref,
    in_sem,
    sums_ref,
    cols,
    grown,
    keys_t,
    scores,
    own,
    inner_ref,
    up_recv,
    up_out,
    dn_recv,
    dn_out,
    final,
    vals,
    small,
    pad,
    dec_d,
    dec_add,
    dec_cv,
    dec_k,
    dec_q,
    up_ss,
    up_rs,
    dn_ss,
    dn_rs,
    f_ss,
    f_rs,
    v_ss,
    v_rs,
    m_ss,
    m_rs,
):
    g = lax.axis_index("groups")
    s = lax.axis_index("seq")
    b = lax.axis_index("beam")
    toks, width = x_ref.shape
    n = keys_ref.shape[1]
    chunks = width // LANES
    _, steps, dwidth = sv_ref.shape
    dheads = dwidth // P_SIZE
    dchunks = dwidth // LANES
    last = ns - 1

    loads = [
        pltpu.make_async_copy(source, here, in_sem.at[i])
        for i, (source, here) in enumerate(
            (
                (decay_in, decay_ref),
                (keys_in, keys_ref),
                (x_in, x_ref),
                (fin_in, fin_ref),
                (sd_in, sd_ref),
                (sv_in, sv_ref),
                (sk_in, sk_ref),
                (lp_in, lp_ref),
                (par_in, par_ref),
                (queries_in, queries_ref),
                (sq_in, sq_ref),
                (len_in, len_ref),
                (score_in, score_ref),
            )
        )
    ]
    for load in loads:
        load.start()

    barrier = pltpu.get_barrier_semaphore()

    def peer(i):
        return lax.rem(b + i, nb)

    @pl.when(s > 0)
    def _():
        pl.semaphore_signal(barrier, inc=1, device_id=(g, s - 1, b), device_id_type=MESH)

    @pl.when(s < last)
    def _():
        pl.semaphore_signal(barrier, inc=1, device_id=(g, s + 1, b), device_id_type=MESH)

    for i in range(1, nb):
        pl.semaphore_signal(barrier, inc=1, device_id=(g, s, peer(i)), device_id_type=MESH)

    def lanes_of(k):
        return pl.ds(pl.multiple_of(k * LANES, LANES), LANES)

    piece = n // PIECES

    def up_rows(p, top=0):
        return pl.ds(top + p * piece, piece)

    def dn_rows(p):
        return pl.ds(0, ROWS + piece) if p == 0 else up_rows(p, ROWS)

    def up_copy(src, k, p):
        return pltpu.make_async_remote_copy(
            src_ref=src,
            dst_ref=up_recv.at[k, up_rows(p)],
            send_sem=up_ss.at[k, p],
            recv_sem=up_rs.at[k, p],
            device_id=(g, lax.rem(s + 1, ns), b),
            device_id_type=MESH,
        )

    def up_sent(k, p):
        return up_copy(up_out.at[k, up_rows(p)], k, p)

    def dn_copy(src, k, p):
        return pltpu.make_async_remote_copy(
            src_ref=src.at[k, dn_rows(p)],
            dst_ref=dn_recv.at[k, dn_rows(p)],
            send_sem=dn_ss.at[k, p],
            recv_sem=dn_rs.at[k, p],
            device_id=(g, lax.rem(s + ns - 1, ns), b),
            device_id_type=MESH,
        )

    owner = (s * dchunks) // chunks
    mates = nb // CORES
    chip, core = b // CORES, lax.rem(b, CORES)
    other_core = chip * CORES + (CORES - 1 - core)
    is_owner = b == owner
    relays = (core == lax.rem(owner, CORES)) & (b != owner)
    near = relays | (chip == owner // CORES)

    def f_copy(kk, i):
        to = other_core if i == 0 else lax.rem(chip + i, mates) * CORES + core
        return pltpu.make_async_remote_copy(
            src_ref=final.at[kk],
            dst_ref=final.at[kk],
            send_sem=f_ss.at[kk, i],
            recv_sem=f_rs.at[kk],
            device_id=(g, s, to),
            device_id_type=MESH,
        )

    def v_copy(i):
        return pltpu.make_async_remote_copy(
            src_ref=vals.at[b],
            dst_ref=vals.at[b],
            send_sem=v_ss.at[i - 1],
            recv_sem=v_rs.at[i - 1],
            device_id=(g, s, peer(i)),
            device_id_type=MESH,
        )

    def m_copy(i):
        return pltpu.make_async_remote_copy(
            src_ref=small.at[b],
            dst_ref=small.at[b],
            send_sem=m_ss.at[i - 1],
            recv_sem=m_rs.at[i - 1],
            device_id=(g, s, peer(i)),
            device_id_type=MESH,
        )

    def target(k):
        return (b * chunks + k) // dchunks

    def place(k):
        return lax.rem(b * chunks + k, dchunks)

    for load in loads[:3]:
        load.wait()

    row_id = lax.broadcasted_iota(jnp.int32, (toks, toks), 0)
    col_id = lax.broadcasted_iota(jnp.int32, (toks, toks), 1)
    upper = (row_id <= col_id).astype(F32).astype(BF16)
    parts = split3(decay_ref[...] * LOG2E)
    sums_ref[...] = sum(mm(part, upper) for part in reversed(parts))
    keys_t[...] = keys_ref[...].astype(F32).T.astype(BF16)

    left = lax.broadcasted_iota(jnp.int32, (1, LANES), 1) < P_SIZE

    def make_column(head):
        row = sums_ref[pl.ds(head, 1), :]
        column = jnp.broadcast_to(row, (LANES, toks)).T
        cols[head] = column
        return column

    def make_state(k, carry):
        column = jnp.where(left, make_column(k * PAIR), make_column(k * PAIR + 1))
        end = column[toks - 1 : toks, :]
        scaled = (x_ref[:, lanes_of(k)].astype(F32) * jnp.exp2(end - column)).astype(BF16)
        own[k, ROWS : ROWS + n, :] = mm(keys_t[...], scaled)
        grown[k] = jnp.exp2(column)
        own[k, 0:ROWS, :] = jnp.broadcast_to(jnp.exp2(end), (ROWS, LANES))
        return carry

    make_state(0, 0)

    met = nb - 1 + jnp.where(s > 0, 1, 0) + jnp.where(s < last, 1, 0)
    pl.semaphore_wait(barrier, met)

    def first_sends(k):
        @pl.when((s == 0) & (s < last))
        def _():
            for p in range(PIECES):
                up_copy(own.at[k, up_rows(p, ROWS)], k, p).start()

        @pl.when((s == last) & (s > target(k)))
        def _():
            for p in range(PIECES):
                dn_copy(own, k, p).start()

    first_sends(0)

    def state_and_send(k, carry):
        make_state(k, 0)
        first_sends(k)
        return carry

    at_edge = (s == 0) | (s == last)

    @pl.when(at_edge)
    def _():
        lax.fori_loop(1, chunks, state_and_send, 0)

    for load in loads[3:]:
        load.wait()

    def column_of(row):
        row = row.astype(F32)
        pad[...] = jnp.zeros_like(pad)
        for step in range(steps):
            pad[step : step + 1, :] = jnp.broadcast_to(row[:, step : step + 1], (1, LANES))
        return pad[0:steps, :]

    live = 1.0 - column_of(fin_ref[...])
    chance = column_of(lp_ref[...]) * live
    parent_of = column_of(par_ref[...])
    pad[...] = jnp.zeros_like(pad)
    pad[0:steps, 0:dheads] = sd_ref[:, 0, :] * live[:, 0:1] * LOG2E
    spread = (
        lax.broadcasted_iota(jnp.int32, (LANES, dwidth), 0)
        == lax.broadcasted_iota(jnp.int32, (LANES, dwidth), 1) // P_SIZE
    )
    spread = spread.astype(F32).astype(BF16)
    wide = sum(mm(part, spread) for part in reversed(split3(pad[...])))
    vals[b, 0:steps, :] = sv_ref[0].astype(F32) * live[:, 0:1]
    vals[b, steps : 2 * steps, :] = wide[0:steps, :]
    small[b] = jnp.zeros(small.shape[1:], F32)
    small[b, 0:steps, :] = sk_ref[0].astype(F32)
    small[b, steps : 2 * steps, :] = parent_of
    small[b, 2 * steps : 3 * steps, :] = chance
    small[b, 3 * steps : 4 * steps, :] = live
    small[b, 4 * steps : 4 * steps + 1, :] = jnp.full((1, LANES), score_ref[0], F32)
    small[b, 4 * steps + 1 : 4 * steps + 2, :] = jnp.full((1, LANES), len_ref[0], jnp.int32).astype(F32)

    for i in range(1, nb):
        m_copy(i).start()
        v_copy(i).start()

    scores[...] = jnp.where(row_id >= col_id, mm(queries_ref[...], keys_t[...]), 0.0)

    pad[...] = jnp.zeros_like(pad)
    pad[0:steps, :] = live
    dec_d[...] = jnp.zeros_like(dec_d)
    dec_add[...] = jnp.zeros_like(dec_add)
    dec_cv[...] = jnp.zeros_like(dec_cv)
    dec_k[...] = jnp.zeros_like(dec_k)
    dec_q[...] = jnp.zeros_like(dec_q)
    dec_q[0:steps, :] = sq_ref[0].astype(F32)
    own_slot = [jnp.where(b == slot, jnp.ones((1, LANES), F32), 0.0) for slot in range(nb)]

    def pick(weights, ref, row):
        total = None
        for slot in range(nb):
            value = ref[slot, row : row + 1, :]
            weight = weights[slot] if value.shape[1] == LANES else weights[slot][:, 0:1]
            total = weight * value if total is None else total + weight * value
        return total

    def prepare(step):
        chain = own_slot
        decay = jnp.zeros((1, dwidth), F32)
        added = jnp.zeros((1, dwidth), F32)
        query = dec_q[step : step + 1, :]
        for t in range(step, -1, -1):
            value = jnp.exp2(decay) * pick(chain, vals, t)
            key = pick(chain, small, t)
            added = added + jnp.sum(key * query, axis=1, keepdims=True) * value
            decay = decay + pick(chain, vals, steps + t)
            if step == steps - 1:
                high = value.astype(BF16).astype(F32)
                dec_cv[t : t + 1, :] = high
                dec_cv[ROWS + t : ROWS + t + 1, :] = value - high
                dec_k[t : t + 1, :] = key
                dec_k[ROWS + t : ROWS + t + 1, :] = key
            if t > 0:
                parent = pick(chain, small, steps + t)
                chain = [jnp.where(parent == float(slot), 1.0, 0.0) for slot in range(nb)]
        open_now = pad[step : step + 1, 0:1]
        dec_d[step : step + 1, :] = jnp.exp2(decay)
        dec_add[step : step + 1, :] = added * open_now

    def rank_slots():
        score = [small[slot, 4 * steps : 4 * steps + 1, :] for slot in range(nb)]
        length = [small[slot, 4 * steps + 1 : 4 * steps + 2, :] for slot in range(nb)]
        for step in range(steps):
            new_score, new_length, normed = [], [], []
            for slot in range(nb):
                parent = small[slot, steps + step : steps + step + 1, :]
                picked_score, picked_length = score[0], length[0]
                for other in range(1, nb):
                    picked_score = jnp.where(parent == float(other), score[other], picked_score)
                    picked_length = jnp.where(parent == float(other), length[other], picked_length)
                new_score.append(picked_score + small[slot, 2 * steps + step : 2 * steps + step + 1, :])
                new_length.append(picked_length + small[slot, 3 * steps + step : 3 * steps + step + 1, :])
                normed.append(new_score[-1] / jnp.exp(0.6 * jnp.log((5.0 + new_length[-1]) / 6.0)))
            score, length = new_score, new_length
            best = functools.reduce(jnp.maximum, normed)
            mine = sum(own_slot[slot] * normed[slot] for slot in range(nb))
            rank_ref[:, step : step + 1] = (mine - best)[:, 0:1]

    def forward_down(k):
        for p in range(PIECES):
            dn_copy(dn_out, k, p).wait_recv()
            shrink = dn_recv[k, 0:1, :]
            rows = up_rows(p, ROWS)
            if p == 0:
                dn_out[k, 0:ROWS, :] = dn_recv[k, 0:ROWS, :] * own[k, 0:ROWS, :]
            dn_out[k, rows, :] = dn_recv[k, rows, :] + shrink * own[k, rows, :]
            dn_copy(dn_out, k, p).start()

    def finish(kk):
        at = lanes_of(kk)
        state = final[kk]
        read = mm(dec_q[...].astype(BF16), state.astype(BF16))
        keep = pad[:, 0:1]
        dec_add[:, at] = keep * (dec_d[:, at] * read) + dec_add[:, at]
        outer = mm_first(dec_cv[:, at].astype(BF16), dec_k[...].astype(BF16))
        rows = pl.ds(pl.multiple_of(kk * LANES, LANES), LANES)
        beam_ref[0, rows, :] = (state * dec_d[steps - 1 : steps, at]).T + outer

    def await_and_finish(kk):
        @pl.when(b != owner)
        def _():
            f_copy(kk, 0).wait_recv()

        @pl.when(relays)
        def _():
            f_copy(kk, 0).start()

        finish(kk)

    up_lag = s * HOP
    dn_lag = (last - s) * HOP
    own_lag = jnp.maximum(jnp.maximum(up_lag, dn_lag), START + steps)
    first = lax.rem(s * dchunks, chunks)
    slots = chunks + max(last * HOP, START + steps) + SHARE

    def inside(k):
        return (k >= 0) & (k < chunks)

    def make_inner(k):
        values = x_ref[:, lanes_of(k)]
        for i in range(toks // LANES):
            at = slice(i * LANES, (i + 1) * LANES)
            until = (i + 1) * LANES
            made = []
            for j in range(PAIR):
                row = sums_ref[pl.ds(k * PAIR + j, 1), :]
                col = cols[k * PAIR + j, at, :]
                blocks = []
                for other in range(i + 1):
                    to = slice(other * LANES, (other + 1) * LANES)
                    gap = jnp.minimum(col - row[:, to], 0.0)
                    blocks.append((scores[at, to] * jnp.exp2(gap)).astype(BF16))
                weights = blocks[0] if i == 0 else jnp.concatenate(blocks, axis=1)
                made.append(mm(weights, values[0:until, :]))
            inner_ref[k, at, :] = jnp.where(left, made[0], made[1])

    def take_up(k):
        @pl.when(s == 0)
        def _():
            up_out[k] = own[k, ROWS : ROWS + n, :]
            out_ref[:, lanes_of(k)] = inner_ref[k].astype(BF16)

        @pl.when(s > 0)
        def _():
            for p in range(PIECES):
                up_sent(k, p).wait_recv()
                up_out[k, up_rows(p), :] = (
                    own[k, 0:1, :] * up_recv[k, up_rows(p), :] + own[k, up_rows(p, ROWS), :]
                )

                @pl.when(s < last)
                def _():
                    up_sent(k, p).start()

            carried = mm(queries_ref[...], up_recv[k].astype(BF16)) * grown[k]
            out_ref[:, lanes_of(k)] = (inner_ref[k] + carried).astype(BF16)

    def share_final(k):
        kk = place(k)

        @pl.when(s < last)
        def _():
            for p in range(PIECES):
                dn_copy(dn_out, k, p).wait_recv()
            final[kk] = dn_recv[k, 0:1, :] * up_out[k] + dn_recv[k, ROWS : ROWS + n, :]

        @pl.when(s == last)
        def _():
            final[kk] = up_out[k]

        for i in range(mates):
            f_copy(kk, i).start()

    def body(slot, carry):
        for step in range(steps):

            @pl.when(slot == START + step)
            def _():
                if step == 0:
                    for i in range(1, nb):
                        m_copy(i).wait_recv()
                        v_copy(i).wait_recv()
                prepare(step)

        @pl.when((slot > 0) & (slot < chunks) & (s > 0) & (s < last))
        def _():
            make_state(slot, 0)

        @pl.when(slot < chunks)
        def _():
            make_inner(slot)

        down = slot - dn_lag
        goes_down = inside(down) & (s > target(down)) & (s < last)

        @pl.when(goes_down & (2 * s >= ns))
        def _():
            forward_down(down)

        @pl.when(inside(slot - up_lag))
        def _():
            take_up(slot - up_lag)

        @pl.when(goes_down & (2 * s < ns))
        def _():
            forward_down(down)

        at_end = slot - own_lag

        @pl.when(inside(at_end) & (s == target(at_end)))
        def _():
            share_final(at_end)

        kk = slot - own_lag - first - jnp.where(is_owner, 0, jnp.where(near, RELAY, SHARE))

        @pl.when((kk >= 0) & (kk < dchunks))
        def _():
            await_and_finish(kk)

        return carry

    lax.fori_loop(0, slots, body, 0)
    rank_slots()
    for step in range(steps):
        so_ref[:, step : step + 1, :] = dec_add[step : step + 1, :].astype(BF16)[None]

    for i in range(1, nb):
        m_copy(i).wait_send()
        v_copy(i).wait_send()

    def drain(k, carry):
        @pl.when(s < last)
        def _():
            for p in range(PIECES):
                up_sent(k, p).wait_send()

        @pl.when(s > target(k))
        def _():
            for p in range(PIECES):
                dn_copy(dn_out, k, p).wait_send()

        @pl.when(s == target(k))
        def _():
            for i in range(mates):
                f_copy(place(k), i).wait_send()

        return carry

    lax.fori_loop(0, chunks, drain, 0)

    @pl.when(relays)
    def _():
        def drain_relay(kk, carry):
            f_copy(kk, 0).wait_send()
            return carry

        lax.fori_loop(0, dchunks, drain_relay, 0)


def on_device(ns, nb, *args):
    x, keys, queries, decay, sv, sk, sq, sd, lp, par, fin, lens, score = args
    toks, width = x.shape
    n = keys.shape[1]
    heads = decay.shape[1]
    steps, _, dwidth = sv.shape
    chunks, dchunks = width // LANES, dwidth // LANES
    small_rows = -(-(4 * steps + 2) // ROWS) * ROWS
    dma = pltpu.SemaphoreType.DMA
    spec = pl.BlockSpec(memory_space=pltpu.VMEM)
    outside = pl.BlockSpec(memory_space=pl.ANY)
    peers = max(nb - 1, 1)
    turn = lambda a: jnp.transpose(a, (1, 0, 2))
    inputs = (x, keys, queries, decay.T, turn(sv), turn(sk), turn(sq), sd, lp.T, par.T, fin.T, lens, score)
    prompt, step_out, ranked, states = pl.pallas_call(
        functools.partial(kernel, ns, nb),
        out_shape=(
            jax.ShapeDtypeStruct((toks, width), BF16),
            jax.ShapeDtypeStruct((1, steps, dwidth), BF16),
            jax.ShapeDtypeStruct((1, steps), F32),
            jax.ShapeDtypeStruct((1, dwidth, n), F32),
        ),
        in_specs=[outside] * 13,
        out_specs=(spec,) * 4,
        scratch_shapes=[
            *[pltpu.VMEM(a.shape, a.dtype) for a in inputs[:11]],
            *[pltpu.SMEM(a.shape, a.dtype) for a in inputs[11:]],
            dma((len(inputs),)),
            pltpu.VMEM((heads, toks), F32),
            pltpu.VMEM((heads, toks, LANES), F32),
            pltpu.VMEM((chunks, toks, LANES), F32),
            pltpu.VMEM((n, toks), BF16),
            pltpu.VMEM((toks, toks), F32),
            pltpu.VMEM((chunks, n + ROWS, LANES), F32),
            pltpu.VMEM((chunks, toks, LANES), F32),
            pltpu.VMEM((chunks, n, LANES), F32),
            pltpu.VMEM((chunks, n, LANES), F32),
            pltpu.VMEM((chunks, n + ROWS, LANES), F32),
            pltpu.VMEM((chunks, n + ROWS, LANES), F32),
            pltpu.VMEM((dchunks, n, LANES), F32),
            pltpu.VMEM((nb, 2 * steps, dwidth), F32),
            pltpu.VMEM((nb, small_rows, LANES), F32),
            pltpu.VMEM((ROWS, LANES), F32),
            pltpu.VMEM((ROWS, dwidth), F32),
            pltpu.VMEM((ROWS, dwidth), F32),
            pltpu.VMEM((2 * ROWS, dwidth), F32),
            pltpu.VMEM((2 * ROWS, n), F32),
            pltpu.VMEM((ROWS, n), F32),
            dma((chunks, PIECES)),
            dma((chunks, PIECES)),
            dma((chunks, PIECES)),
            dma((chunks, PIECES)),
            dma((dchunks, nb // CORES)),
            dma((dchunks,)),
            dma((peers,)),
            dma((peers,)),
            dma((peers,)),
            dma((peers,)),
        ],
        compiler_params=pltpu.CompilerParams(
            collective_id=0, has_side_effects=True, vmem_limit_bytes=60 * 1024 * 1024
        ),
    )(*inputs)
    return prompt, turn(step_out), ranked.T, states


def solution(mesh):
    return jax.shard_map(
        functools.partial(on_device, mesh.shape["seq"], mesh.shape["beam"]),
        mesh=mesh,
        in_specs=(
            P(("groups", "seq"), "beam"),
            P(("groups", "seq"), None),
            P(("groups", "seq"), None),
            P(("groups", "seq"), "beam"),
            P("groups", "beam", "seq"),
            P("groups", "beam", None),
            P("groups", "beam", None),
            P("groups", "beam", "seq"),
            P("groups", "beam"),
            P("groups", "beam"),
            P("groups", "beam"),
            P(("groups", "beam")),
            P(("groups", "beam")),
        ),
        out_specs=(
            P(("groups", "seq"), "beam"),
            P("groups", "beam", "seq"),
            P("groups", "beam"),
            P(("groups", "beam"), "seq", None),
        ),
        check_vma=False,
    )
```

```python
import functools
import math

import jax
import jax.numpy as jnp
from jax import lax
from jax.experimental import pallas as pl
from jax.experimental.pallas import tpu as pltpu
from jax.sharding import PartitionSpec as P

P_SIZE = 64
LANES = 128
PAIR = LANES // P_SIZE
ROWS = 8
HOP = 3
RELAY = 3
SHARE = 6
START = 4
CORES = 2
PIECES = 1
LOG2E = math.log2(math.e)
MESH = pl.DeviceIdType.MESH
F32 = jnp.float32
BF16 = jnp.bfloat16


def split3(x):
    first = x.astype(BF16)
    rest = x - first.astype(F32)
    second = rest.astype(BF16)
    return first, second, (rest - second.astype(F32)).astype(BF16)


def mm(a, b):
    return jnp.dot(a, b, preferred_element_type=F32)


def mm_first(a, b):
    return lax.dot_general(a, b, (((0,), (0,)), ((), ())), preferred_element_type=F32)


def kernel(
    ns,
    nb,
    x_in,
    keys_in,
    queries_in,
    decay_in,
    sv_in,
    sk_in,
    sq_in,
    sd_in,
    lp_in,
    par_in,
    fin_in,
    len_in,
    score_in,
    out_ref,
    so_ref,
    rank_ref,
    beam_ref,
    x_ref,
    keys_ref,
    queries_ref,
    decay_ref,
    sv_ref,
    sk_ref,
    sq_ref,
    sd_ref,
    lp_ref,
    par_ref,
    fin_ref,
    len_ref,
    score_ref,
    in_sem,
    sums_ref,
    cols,
    grown,
    keys_t,
    scores,
    own,
    inner_ref,
    up_recv,
    up_out,
    dn_recv,
    dn_out,
    final,
    vals,
    small,
    pad,
    dec_d,
    dec_add,
    dec_cv,
    dec_k,
    dec_q,
    up_ss,
    up_rs,
    dn_ss,
    dn_rs,
    f_ss,
    f_rs,
    v_ss,
    v_rs,
    m_ss,
    m_rs,
):
    g = lax.axis_index("groups")
    s = lax.axis_index("seq")
    b = lax.axis_index("beam")
    toks, width = x_ref.shape
    n = keys_ref.shape[1]
    chunks = width // LANES
    _, steps, dwidth = sv_ref.shape
    dheads = dwidth // P_SIZE
    dchunks = dwidth // LANES
    last = ns - 1

    loads = [
        pltpu.make_async_copy(source, here, in_sem.at[i])
        for i, (source, here) in enumerate(
            (
                (decay_in, decay_ref),
                (keys_in, keys_ref),
                (x_in, x_ref),
                (fin_in, fin_ref),
                (sd_in, sd_ref),
                (sv_in, sv_ref),
                (sk_in, sk_ref),
                (lp_in, lp_ref),
                (par_in, par_ref),
                (queries_in, queries_ref),
                (sq_in, sq_ref),
                (len_in, len_ref),
                (score_in, score_ref),
            )
        )
    ]
    for load in loads:
        load.start()

    barrier = pltpu.get_barrier_semaphore()

    def peer(i):
        return lax.rem(b + i, nb)

    @pl.when(s > 0)
    def _():
        pl.semaphore_signal(barrier, inc=1, device_id=(g, s - 1, b), device_id_type=MESH)

    @pl.when(s < last)
    def _():
        pl.semaphore_signal(barrier, inc=1, device_id=(g, s + 1, b), device_id_type=MESH)

    for i in range(1, nb):
        pl.semaphore_signal(barrier, inc=1, device_id=(g, s, peer(i)), device_id_type=MESH)

    def lanes_of(k):
        return pl.ds(pl.multiple_of(k * LANES, LANES), LANES)

    piece = n // PIECES

    def up_rows(p, top=0):
        return pl.ds(top + p * piece, piece)

    def dn_rows(p):
        return pl.ds(0, ROWS + piece) if p == 0 else up_rows(p, ROWS)

    def up_copy(src, k, p):
        return pltpu.make_async_remote_copy(
            src_ref=src,
            dst_ref=up_recv.at[k, up_rows(p)],
            send_sem=up_ss.at[k, p],
            recv_sem=up_rs.at[k, p],
            device_id=(g, lax.rem(s + 1, ns), b),
            device_id_type=MESH,
        )

    def up_sent(k, p):
        return up_copy(up_out.at[k, up_rows(p)], k, p)

    def dn_copy(src, k, p):
        return pltpu.make_async_remote_copy(
            src_ref=src.at[k, dn_rows(p)],
            dst_ref=dn_recv.at[k, dn_rows(p)],
            send_sem=dn_ss.at[k, p],
            recv_sem=dn_rs.at[k, p],
            device_id=(g, lax.rem(s + ns - 1, ns), b),
            device_id_type=MESH,
        )

    owner = (s * dchunks) // chunks
    mates = nb // CORES
    chip, core = b // CORES, lax.rem(b, CORES)
    other_core = chip * CORES + (CORES - 1 - core)
    is_owner = b == owner
    relays = (core == lax.rem(owner, CORES)) & (b != owner)
    near = relays | (chip == owner // CORES)

    def f_copy(kk, i):
        to = other_core if i == 0 else lax.rem(chip + i, mates) * CORES + core
        return pltpu.make_async_remote_copy(
            src_ref=final.at[kk],
            dst_ref=final.at[kk],
            send_sem=f_ss.at[kk, i],
            recv_sem=f_rs.at[kk],
            device_id=(g, s, to),
            device_id_type=MESH,
        )

    def v_copy(i):
        return pltpu.make_async_remote_copy(
            src_ref=vals.at[b],
            dst_ref=vals.at[b],
            send_sem=v_ss.at[i - 1],
            recv_sem=v_rs.at[i - 1],
            device_id=(g, s, peer(i)),
            device_id_type=MESH,
        )

    def m_copy(i):
        return pltpu.make_async_remote_copy(
            src_ref=small.at[b],
            dst_ref=small.at[b],
            send_sem=m_ss.at[i - 1],
            recv_sem=m_rs.at[i - 1],
            device_id=(g, s, peer(i)),
            device_id_type=MESH,
        )

    def target(k):
        return (b * chunks + k) // dchunks

    def place(k):
        return lax.rem(b * chunks + k, dchunks)

    for load in loads[:3]:
        load.wait()

    row_id = lax.broadcasted_iota(jnp.int32, (toks, toks), 0)
    col_id = lax.broadcasted_iota(jnp.int32, (toks, toks), 1)
    upper = (row_id <= col_id).astype(F32).astype(BF16)
    parts = split3(decay_ref[...] * LOG2E)
    sums_ref[...] = sum(mm(part, upper) for part in reversed(parts))
    keys_t[...] = keys_ref[...].astype(F32).T.astype(BF16)

    left = lax.broadcasted_iota(jnp.int32, (1, LANES), 1) < P_SIZE

    def make_column(head):
        row = sums_ref[pl.ds(head, 1), :]
        column = jnp.broadcast_to(row, (LANES, toks)).T
        cols[head] = column
        return column

    def make_state(k, carry):
        column = jnp.where(left, make_column(k * PAIR), make_column(k * PAIR + 1))
        end = column[toks - 1 : toks, :]
        scaled = (x_ref[:, lanes_of(k)].astype(F32) * jnp.exp2(end - column)).astype(BF16)
        own[k, ROWS : ROWS + n, :] = mm(keys_t[...], scaled)
        grown[k] = jnp.exp2(column)
        own[k, 0:ROWS, :] = jnp.broadcast_to(jnp.exp2(end), (ROWS, LANES))
        return carry

    make_state(0, 0)

    met = nb - 1 + jnp.where(s > 0, 1, 0) + jnp.where(s < last, 1, 0)
    pl.semaphore_wait(barrier, met)

    def first_sends(k):
        @pl.when((s == 0) & (s < last))
        def _():
            for p in range(PIECES):
                up_copy(own.at[k, up_rows(p, ROWS)], k, p).start()

        @pl.when((s == last) & (s > target(k)))
        def _():
            for p in range(PIECES):
                dn_copy(own, k, p).start()

    first_sends(0)

    together = 2 if chunks % 2 == 0 else 1

    def state_and_send(group, carry):
        for i in range(together):
            make_state(group * together + i, 0)
        for i in range(together):
            first_sends(group * together + i)
        return carry

    at_edge = (s == 0) | (s == last)

    @pl.when(at_edge)
    def _():
        for i in range(1, together):
            make_state(i, 0)
            first_sends(i)
        lax.fori_loop(1, chunks // together, state_and_send, 0)

    for load in loads[3:]:
        load.wait()

    def column_of(row):
        row = row.astype(F32)
        pad[...] = jnp.zeros_like(pad)
        for step in range(steps):
            pad[step : step + 1, :] = jnp.broadcast_to(row[:, step : step + 1], (1, LANES))
        return pad[0:steps, :]

    live = 1.0 - column_of(fin_ref[...])
    chance = column_of(lp_ref[...]) * live
    parent_of = column_of(par_ref[...])
    pad[...] = jnp.zeros_like(pad)
    pad[0:steps, 0:dheads] = sd_ref[:, 0, :] * live[:, 0:1] * LOG2E
    spread = (
        lax.broadcasted_iota(jnp.int32, (LANES, dwidth), 0)
        == lax.broadcasted_iota(jnp.int32, (LANES, dwidth), 1) // P_SIZE
    )
    spread = spread.astype(F32).astype(BF16)
    wide = sum(mm(part, spread) for part in reversed(split3(pad[...])))
    vals[b, 0:steps, :] = sv_ref[0].astype(F32) * live[:, 0:1]
    vals[b, steps : 2 * steps, :] = wide[0:steps, :]
    small[b] = jnp.zeros(small.shape[1:], F32)
    small[b, 0:steps, :] = sk_ref[0].astype(F32)
    small[b, steps : 2 * steps, :] = parent_of
    small[b, 2 * steps : 3 * steps, :] = chance
    small[b, 3 * steps : 4 * steps, :] = live
    small[b, 4 * steps : 4 * steps + 1, :] = jnp.full((1, LANES), score_ref[0], F32)
    small[b, 4 * steps + 1 : 4 * steps + 2, :] = jnp.full((1, LANES), len_ref[0], jnp.int32).astype(F32)

    for i in range(1, nb):
        m_copy(i).start()
        v_copy(i).start()

    scores[...] = jnp.where(row_id >= col_id, mm(queries_ref[...], keys_t[...]), 0.0)

    pad[...] = jnp.zeros_like(pad)
    pad[0:steps, :] = live
    dec_d[...] = jnp.zeros_like(dec_d)
    dec_add[...] = jnp.zeros_like(dec_add)
    dec_cv[...] = jnp.zeros_like(dec_cv)
    dec_k[...] = jnp.zeros_like(dec_k)
    dec_q[...] = jnp.zeros_like(dec_q)
    dec_q[0:steps, :] = sq_ref[0].astype(F32)
    own_slot = [jnp.where(b == slot, jnp.ones((1, LANES), F32), 0.0) for slot in range(nb)]

    def pick(weights, ref, row):
        total = None
        for slot in range(nb):
            value = ref[slot, row : row + 1, :]
            weight = weights[slot] if value.shape[1] == LANES else weights[slot][:, 0:1]
            total = weight * value if total is None else total + weight * value
        return total

    def prepare(step):
        chain = own_slot
        decay = jnp.zeros((1, dwidth), F32)
        added = jnp.zeros((1, dwidth), F32)
        query = dec_q[step : step + 1, :]
        for t in range(step, -1, -1):
            value = jnp.exp2(decay) * pick(chain, vals, t)
            key = pick(chain, small, t)
            added = added + jnp.sum(key * query, axis=1, keepdims=True) * value
            decay = decay + pick(chain, vals, steps + t)
            if step == steps - 1:
                high = value.astype(BF16).astype(F32)
                dec_cv[t : t + 1, :] = high
                dec_cv[ROWS + t : ROWS + t + 1, :] = value - high
                dec_k[t : t + 1, :] = key
                dec_k[ROWS + t : ROWS + t + 1, :] = key
            if t > 0:
                parent = pick(chain, small, steps + t)
                chain = [jnp.where(parent == float(slot), 1.0, 0.0) for slot in range(nb)]
        open_now = pad[step : step + 1, 0:1]
        dec_d[step : step + 1, :] = jnp.exp2(decay)
        dec_add[step : step + 1, :] = added * open_now

    def rank_slots():
        score = [small[slot, 4 * steps : 4 * steps + 1, :] for slot in range(nb)]
        length = [small[slot, 4 * steps + 1 : 4 * steps + 2, :] for slot in range(nb)]
        for step in range(steps):
            new_score, new_length, normed = [], [], []
            for slot in range(nb):
                parent = small[slot, steps + step : steps + step + 1, :]
                picked_score, picked_length = score[0], length[0]
                for other in range(1, nb):
                    picked_score = jnp.where(parent == float(other), score[other], picked_score)
                    picked_length = jnp.where(parent == float(other), length[other], picked_length)
                new_score.append(picked_score + small[slot, 2 * steps + step : 2 * steps + step + 1, :])
                new_length.append(picked_length + small[slot, 3 * steps + step : 3 * steps + step + 1, :])
                normed.append(new_score[-1] / jnp.exp(0.6 * jnp.log((5.0 + new_length[-1]) / 6.0)))
            score, length = new_score, new_length
            best = functools.reduce(jnp.maximum, normed)
            mine = sum(own_slot[slot] * normed[slot] for slot in range(nb))
            rank_ref[:, step : step + 1] = (mine - best)[:, 0:1]

    def forward_down(k):
        for p in range(PIECES):
            dn_copy(dn_out, k, p).wait_recv()
            shrink = dn_recv[k, 0:1, :]
            rows = up_rows(p, ROWS)
            if p == 0:
                dn_out[k, 0:ROWS, :] = dn_recv[k, 0:ROWS, :] * own[k, 0:ROWS, :]
            dn_out[k, rows, :] = dn_recv[k, rows, :] + shrink * own[k, rows, :]
            dn_copy(dn_out, k, p).start()

    def finish(kk):
        at = lanes_of(kk)
        state = final[kk]
        read = mm(dec_q[...].astype(BF16), state.astype(BF16))
        keep = pad[:, 0:1]
        dec_add[:, at] = keep * (dec_d[:, at] * read) + dec_add[:, at]
        outer = mm_first(dec_cv[:, at].astype(BF16), dec_k[...].astype(BF16))
        rows = pl.ds(pl.multiple_of(kk * LANES, LANES), LANES)
        beam_ref[0, rows, :] = (state * dec_d[steps - 1 : steps, at]).T + outer

    def await_and_finish(kk):
        @pl.when(b != owner)
        def _():
            f_copy(kk, 0).wait_recv()

        @pl.when(relays)
        def _():
            f_copy(kk, 0).start()

        finish(kk)

    up_lag = s * HOP
    dn_lag = (last - s) * HOP
    own_lag = jnp.maximum(jnp.maximum(up_lag, dn_lag), START + steps)
    first = lax.rem(s * dchunks, chunks)
    slots = chunks + max(last * HOP, START + steps) + SHARE

    def inside(k):
        return (k >= 0) & (k < chunks)

    def make_inner(k):
        values = x_ref[:, lanes_of(k)]
        for i in range(toks // LANES):
            at = slice(i * LANES, (i + 1) * LANES)
            until = (i + 1) * LANES
            made = []
            for j in range(PAIR):
                row = sums_ref[pl.ds(k * PAIR + j, 1), :]
                col = cols[k * PAIR + j, at, :]
                blocks = []
                for other in range(i + 1):
                    to = slice(other * LANES, (other + 1) * LANES)
                    gap = jnp.minimum(col - row[:, to], 0.0)
                    blocks.append((scores[at, to] * jnp.exp2(gap)).astype(BF16))
                weights = blocks[0] if i == 0 else jnp.concatenate(blocks, axis=1)
                made.append(mm(weights, values[0:until, :]))
            inner_ref[k, at, :] = jnp.where(left, made[0], made[1])

    def take_up(k):
        @pl.when(s == 0)
        def _():
            up_out[k] = own[k, ROWS : ROWS + n, :]
            out_ref[:, lanes_of(k)] = inner_ref[k].astype(BF16)

        @pl.when(s > 0)
        def _():
            for p in range(PIECES):
                up_sent(k, p).wait_recv()
                up_out[k, up_rows(p), :] = (
                    own[k, 0:1, :] * up_recv[k, up_rows(p), :] + own[k, up_rows(p, ROWS), :]
                )

                @pl.when(s < last)
                def _():
                    up_sent(k, p).start()

            carried = mm(queries_ref[...], up_recv[k].astype(BF16)) * grown[k]
            out_ref[:, lanes_of(k)] = (inner_ref[k] + carried).astype(BF16)

    def share_final(k):
        kk = place(k)

        @pl.when(s < last)
        def _():
            for p in range(PIECES):
                dn_copy(dn_out, k, p).wait_recv()
            final[kk] = dn_recv[k, 0:1, :] * up_out[k] + dn_recv[k, ROWS : ROWS + n, :]

        @pl.when(s == last)
        def _():
            final[kk] = up_out[k]

        for i in range(mates):
            f_copy(kk, i).start()

    def body(slot, carry):
        for step in range(steps):

            @pl.when(slot == START + step)
            def _():
                if step == 0:
                    for i in range(1, nb):
                        m_copy(i).wait_recv()
                        v_copy(i).wait_recv()
                prepare(step)

        starts = (slot < chunks) & (lax.rem(slot, together) == 0)

        @pl.when(starts & (s > 0) & (s < last))
        def _():
            for i in range(together):
                make_state(slot + i, 0)

        @pl.when(starts)
        def _():
            for i in range(together):
                make_inner(slot + i)

        down = slot - dn_lag
        goes_down = inside(down) & (s > target(down)) & (s < last)

        @pl.when(goes_down & (2 * s >= ns))
        def _():
            forward_down(down)

        @pl.when(inside(slot - up_lag))
        def _():
            take_up(slot - up_lag)

        @pl.when(goes_down & (2 * s < ns))
        def _():
            forward_down(down)

        at_end = slot - own_lag

        @pl.when(inside(at_end) & (s == target(at_end)))
        def _():
            share_final(at_end)

        kk = slot - own_lag - first - jnp.where(is_owner, 0, jnp.where(near, RELAY, SHARE))

        @pl.when((kk >= 0) & (kk < dchunks))
        def _():
            await_and_finish(kk)

        return carry

    lax.fori_loop(0, slots, body, 0)
    rank_slots()
    for step in range(steps):
        so_ref[:, step : step + 1, :] = dec_add[step : step + 1, :].astype(BF16)[None]

    for i in range(1, nb):
        m_copy(i).wait_send()
        v_copy(i).wait_send()

    def drain(k, carry):
        @pl.when(s < last)
        def _():
            for p in range(PIECES):
                up_sent(k, p).wait_send()

        @pl.when(s > target(k))
        def _():
            for p in range(PIECES):
                dn_copy(dn_out, k, p).wait_send()

        @pl.when(s == target(k))
        def _():
            for i in range(mates):
                f_copy(place(k), i).wait_send()

        return carry

    lax.fori_loop(0, chunks, drain, 0)

    @pl.when(relays)
    def _():
        def drain_relay(kk, carry):
            f_copy(kk, 0).wait_send()
            return carry

        lax.fori_loop(0, dchunks, drain_relay, 0)


def on_device(ns, nb, *args):
    x, keys, queries, decay, sv, sk, sq, sd, lp, par, fin, lens, score = args
    toks, width = x.shape
    n = keys.shape[1]
    heads = decay.shape[1]
    steps, _, dwidth = sv.shape
    chunks, dchunks = width // LANES, dwidth // LANES
    small_rows = -(-(4 * steps + 2) // ROWS) * ROWS
    dma = pltpu.SemaphoreType.DMA
    spec = pl.BlockSpec(memory_space=pltpu.VMEM)
    outside = pl.BlockSpec(memory_space=pl.ANY)
    peers = max(nb - 1, 1)
    turn = lambda a: jnp.transpose(a, (1, 0, 2))
    inputs = (x, keys, queries, decay.T, turn(sv), turn(sk), turn(sq), sd, lp.T, par.T, fin.T, lens, score)
    prompt, step_out, ranked, states = pl.pallas_call(
        functools.partial(kernel, ns, nb),
        out_shape=(
            jax.ShapeDtypeStruct((toks, width), BF16),
            jax.ShapeDtypeStruct((1, steps, dwidth), BF16),
            jax.ShapeDtypeStruct((1, steps), F32),
            jax.ShapeDtypeStruct((1, dwidth, n), F32),
        ),
        in_specs=[outside] * 13,
        out_specs=(spec,) * 4,
        scratch_shapes=[
            *[pltpu.VMEM(a.shape, a.dtype) for a in inputs[:11]],
            *[pltpu.SMEM(a.shape, a.dtype) for a in inputs[11:]],
            dma((len(inputs),)),
            pltpu.VMEM((heads, toks), F32),
            pltpu.VMEM((heads, toks, LANES), F32),
            pltpu.VMEM((chunks, toks, LANES), F32),
            pltpu.VMEM((n, toks), BF16),
            pltpu.VMEM((toks, toks), F32),
            pltpu.VMEM((chunks, n + ROWS, LANES), F32),
            pltpu.VMEM((chunks, toks, LANES), F32),
            pltpu.VMEM((chunks, n, LANES), F32),
            pltpu.VMEM((chunks, n, LANES), F32),
            pltpu.VMEM((chunks, n + ROWS, LANES), F32),
            pltpu.VMEM((chunks, n + ROWS, LANES), F32),
            pltpu.VMEM((dchunks, n, LANES), F32),
            pltpu.VMEM((nb, 2 * steps, dwidth), F32),
            pltpu.VMEM((nb, small_rows, LANES), F32),
            pltpu.VMEM((ROWS, LANES), F32),
            pltpu.VMEM((ROWS, dwidth), F32),
            pltpu.VMEM((ROWS, dwidth), F32),
            pltpu.VMEM((2 * ROWS, dwidth), F32),
            pltpu.VMEM((2 * ROWS, n), F32),
            pltpu.VMEM((ROWS, n), F32),
            dma((chunks, PIECES)),
            dma((chunks, PIECES)),
            dma((chunks, PIECES)),
            dma((chunks, PIECES)),
            dma((dchunks, nb // CORES)),
            dma((dchunks,)),
            dma((peers,)),
            dma((peers,)),
            dma((peers,)),
            dma((peers,)),
        ],
        compiler_params=pltpu.CompilerParams(
            collective_id=0, has_side_effects=True, vmem_limit_bytes=60 * 1024 * 1024
        ),
    )(*inputs)
    return prompt, turn(step_out), ranked.T, states


def solution(mesh):
    return jax.shard_map(
        functools.partial(on_device, mesh.shape["seq"], mesh.shape["beam"]),
        mesh=mesh,
        in_specs=(
            P(("groups", "seq"), "beam"),
            P(("groups", "seq"), None),
            P(("groups", "seq"), None),
            P(("groups", "seq"), "beam"),
            P("groups", "beam", "seq"),
            P("groups", "beam", None),
            P("groups", "beam", None),
            P("groups", "beam", "seq"),
            P("groups", "beam"),
            P("groups", "beam"),
            P("groups", "beam"),
            P(("groups", "beam")),
            P(("groups", "beam")),
        ),
        out_specs=(
            P(("groups", "seq"), "beam"),
            P("groups", "beam", "seq"),
            P("groups", "beam"),
            P(("groups", "beam"), "seq", None),
        ),
        check_vma=False,
    )
```

```python
import functools
import math

import jax
import jax.numpy as jnp
from jax import lax
from jax.experimental import pallas as pl
from jax.experimental.pallas import tpu as pltpu
from jax.sharding import PartitionSpec as P

P_SIZE = 64
LANES = 128
PAIR = LANES // P_SIZE
ROWS = 8
HOP = 3
RELAY = 3
SHARE = 6
START = 4
CORES = 2
PIECES = 1
LOG2E = math.log2(math.e)
MESH = pl.DeviceIdType.MESH
F32 = jnp.float32
BF16 = jnp.bfloat16


def split3(x):
    first = x.astype(BF16)
    rest = x - first.astype(F32)
    second = rest.astype(BF16)
    return first, second, (rest - second.astype(F32)).astype(BF16)


def mm(a, b):
    return jnp.dot(a, b, preferred_element_type=F32)


def mm_first(a, b):
    return lax.dot_general(a, b, (((0,), (0,)), ((), ())), preferred_element_type=F32)


def kernel(
    ns,
    nb,
    x_in,
    keys_in,
    queries_in,
    decay_in,
    sv_in,
    sk_in,
    sq_in,
    sd_in,
    lp_in,
    par_in,
    fin_in,
    len_in,
    score_in,
    out_ref,
    so_ref,
    rank_ref,
    beam_ref,
    x_ref,
    keys_ref,
    queries_ref,
    decay_ref,
    sv_ref,
    sk_ref,
    sq_ref,
    sd_ref,
    lp_ref,
    par_ref,
    fin_ref,
    len_ref,
    score_ref,
    in_sem,
    sums_ref,
    cols,
    grown,
    keys_t,
    scores,
    own,
    inner_ref,
    up_recv,
    up_out,
    dn_recv,
    dn_out,
    final,
    vals,
    small,
    pad,
    dec_d,
    dec_add,
    dec_cv,
    dec_k,
    dec_q,
    up_ss,
    up_rs,
    dn_ss,
    dn_rs,
    f_ss,
    f_rs,
    v_ss,
    v_rs,
    m_ss,
    m_rs,
    out_made,
    beam_made,
    out_sem,
    beam_sem,
):
    g = lax.axis_index("groups")
    s = lax.axis_index("seq")
    b = lax.axis_index("beam")
    toks, width = x_ref.shape
    n = keys_ref.shape[1]
    chunks = width // LANES
    _, steps, dwidth = sv_ref.shape
    dheads = dwidth // P_SIZE
    dchunks = dwidth // LANES
    last = ns - 1

    loads = [
        pltpu.make_async_copy(source, here, in_sem.at[i])
        for i, (source, here) in enumerate(
            (
                (decay_in, decay_ref),
                (keys_in, keys_ref),
                (x_in, x_ref),
                (fin_in, fin_ref),
                (sd_in, sd_ref),
                (sv_in, sv_ref),
                (sk_in, sk_ref),
                (lp_in, lp_ref),
                (par_in, par_ref),
                (queries_in, queries_ref),
                (sq_in, sq_ref),
                (len_in, len_ref),
                (score_in, score_ref),
            )
        )
    ]
    for load in loads:
        load.start()

    barrier = pltpu.get_barrier_semaphore()

    def peer(i):
        return lax.rem(b + i, nb)

    @pl.when(s > 0)
    def _():
        pl.semaphore_signal(barrier, inc=1, device_id=(g, s - 1, b), device_id_type=MESH)

    @pl.when(s < last)
    def _():
        pl.semaphore_signal(barrier, inc=1, device_id=(g, s + 1, b), device_id_type=MESH)

    for i in range(1, nb):
        pl.semaphore_signal(barrier, inc=1, device_id=(g, s, peer(i)), device_id_type=MESH)

    def lanes_of(k):
        return pl.ds(pl.multiple_of(k * LANES, LANES), LANES)

    piece = n // PIECES

    def up_rows(p, top=0):
        return pl.ds(top + p * piece, piece)

    def dn_rows(p):
        return pl.ds(0, ROWS + piece) if p == 0 else up_rows(p, ROWS)

    def up_copy(src, k, p):
        return pltpu.make_async_remote_copy(
            src_ref=src,
            dst_ref=up_recv.at[k, up_rows(p)],
            send_sem=up_ss.at[k, p],
            recv_sem=up_rs.at[k, p],
            device_id=(g, lax.rem(s + 1, ns), b),
            device_id_type=MESH,
        )

    def up_sent(k, p):
        return up_copy(up_out.at[k, up_rows(p)], k, p)

    def dn_copy(src, k, p):
        return pltpu.make_async_remote_copy(
            src_ref=src.at[k, dn_rows(p)],
            dst_ref=dn_recv.at[k, dn_rows(p)],
            send_sem=dn_ss.at[k, p],
            recv_sem=dn_rs.at[k, p],
            device_id=(g, lax.rem(s + ns - 1, ns), b),
            device_id_type=MESH,
        )

    owner = (s * dchunks) // chunks
    mates = nb // CORES
    chip, core = b // CORES, lax.rem(b, CORES)
    other_core = chip * CORES + (CORES - 1 - core)
    is_owner = b == owner
    relays = (core == lax.rem(owner, CORES)) & (b != owner)
    near = relays | (chip == owner // CORES)

    def f_copy(kk, i):
        to = other_core if i == 0 else lax.rem(chip + i, mates) * CORES + core
        return pltpu.make_async_remote_copy(
            src_ref=final.at[kk],
            dst_ref=final.at[kk],
            send_sem=f_ss.at[kk, i],
            recv_sem=f_rs.at[kk],
            device_id=(g, s, to),
            device_id_type=MESH,
        )

    def v_copy(i):
        return pltpu.make_async_remote_copy(
            src_ref=vals.at[b],
            dst_ref=vals.at[b],
            send_sem=v_ss.at[i - 1],
            recv_sem=v_rs.at[i - 1],
            device_id=(g, s, peer(i)),
            device_id_type=MESH,
        )

    def m_copy(i):
        return pltpu.make_async_remote_copy(
            src_ref=small.at[b],
            dst_ref=small.at[b],
            send_sem=m_ss.at[i - 1],
            recv_sem=m_rs.at[i - 1],
            device_id=(g, s, peer(i)),
            device_id_type=MESH,
        )

    def out_copy(k):
        return pltpu.make_async_copy(out_made.at[k], out_ref.at[:, lanes_of(k)], out_sem.at[k])

    def beam_copy(kk):
        rows = pl.ds(pl.multiple_of(kk * LANES, LANES), LANES)
        return pltpu.make_async_copy(beam_made.at[kk], beam_ref.at[0, rows], beam_sem.at[kk])

    def target(k):
        return (b * chunks + k) // dchunks

    def place(k):
        return lax.rem(b * chunks + k, dchunks)

    for load in loads[:3]:
        load.wait()

    row_id = lax.broadcasted_iota(jnp.int32, (toks, toks), 0)
    col_id = lax.broadcasted_iota(jnp.int32, (toks, toks), 1)
    upper = (row_id <= col_id).astype(F32).astype(BF16)
    parts = split3(decay_ref[...] * LOG2E)
    sums_ref[...] = sum(mm(part, upper) for part in reversed(parts))
    keys_t[...] = keys_ref[...].astype(F32).T.astype(BF16)

    left = lax.broadcasted_iota(jnp.int32, (1, LANES), 1) < P_SIZE

    def make_column(head):
        row = sums_ref[pl.ds(head, 1), :]
        column = jnp.broadcast_to(row, (LANES, toks)).T
        cols[head] = column
        return column

    def make_state(k, carry):
        column = jnp.where(left, make_column(k * PAIR), make_column(k * PAIR + 1))
        end = column[toks - 1 : toks, :]
        scaled = (x_ref[:, lanes_of(k)].astype(F32) * jnp.exp2(end - column)).astype(BF16)
        own[k, ROWS : ROWS + n, :] = mm(keys_t[...], scaled)
        grown[k] = jnp.exp2(column)
        own[k, 0:ROWS, :] = jnp.broadcast_to(jnp.exp2(end), (ROWS, LANES))
        return carry

    make_state(0, 0)

    met = nb - 1 + jnp.where(s > 0, 1, 0) + jnp.where(s < last, 1, 0)
    pl.semaphore_wait(barrier, met)

    def first_sends(k):
        @pl.when((s == 0) & (s < last))
        def _():
            for p in range(PIECES):
                up_copy(own.at[k, up_rows(p, ROWS)], k, p).start()

        @pl.when((s == last) & (s > target(k)))
        def _():
            for p in range(PIECES):
                dn_copy(own, k, p).start()

    first_sends(0)

    together = 2 if chunks % 2 == 0 else 1

    def state_and_send(group, carry):
        for i in range(together):
            make_state(group * together + i, 0)
        for i in range(together):
            first_sends(group * together + i)
        return carry

    at_edge = (s == 0) | (s == last)

    @pl.when(at_edge)
    def _():
        for i in range(1, together):
            make_state(i, 0)
            first_sends(i)
        lax.fori_loop(1, chunks // together, state_and_send, 0)

    for load in loads[3:]:
        load.wait()

    def column_of(row):
        row = row.astype(F32)
        pad[...] = jnp.zeros_like(pad)
        for step in range(steps):
            pad[step : step + 1, :] = jnp.broadcast_to(row[:, step : step + 1], (1, LANES))
        return pad[0:steps, :]

    live = 1.0 - column_of(fin_ref[...])
    chance = column_of(lp_ref[...]) * live
    parent_of = column_of(par_ref[...])
    pad[...] = jnp.zeros_like(pad)
    pad[0:steps, 0:dheads] = sd_ref[:, 0, :] * live[:, 0:1] * LOG2E
    spread = (
        lax.broadcasted_iota(jnp.int32, (LANES, dwidth), 0)
        == lax.broadcasted_iota(jnp.int32, (LANES, dwidth), 1) // P_SIZE
    )
    spread = spread.astype(F32).astype(BF16)
    wide = sum(mm(part, spread) for part in reversed(split3(pad[...])))
    vals[b, 0:steps, :] = sv_ref[0].astype(F32) * live[:, 0:1]
    vals[b, steps : 2 * steps, :] = wide[0:steps, :]
    small[b] = jnp.zeros(small.shape[1:], F32)
    small[b, 0:steps, :] = sk_ref[0].astype(F32)
    small[b, steps : 2 * steps, :] = parent_of
    small[b, 2 * steps : 3 * steps, :] = chance
    small[b, 3 * steps : 4 * steps, :] = live
    small[b, 4 * steps : 4 * steps + 1, :] = jnp.full((1, LANES), score_ref[0], F32)
    small[b, 4 * steps + 1 : 4 * steps + 2, :] = jnp.full((1, LANES), len_ref[0], jnp.int32).astype(F32)

    for i in range(1, nb):
        m_copy(i).start()
        v_copy(i).start()

    scores[...] = jnp.where(row_id >= col_id, mm(queries_ref[...], keys_t[...]), 0.0)

    pad[...] = jnp.zeros_like(pad)
    pad[0:steps, :] = live
    dec_d[...] = jnp.zeros_like(dec_d)
    dec_add[...] = jnp.zeros_like(dec_add)
    dec_cv[...] = jnp.zeros_like(dec_cv)
    dec_k[...] = jnp.zeros_like(dec_k)
    dec_q[...] = jnp.zeros_like(dec_q)
    dec_q[0:steps, :] = sq_ref[0].astype(F32)
    own_slot = [jnp.where(b == slot, jnp.ones((1, LANES), F32), 0.0) for slot in range(nb)]

    def pick(weights, ref, row):
        total = None
        for slot in range(nb):
            value = ref[slot, row : row + 1, :]
            weight = weights[slot] if value.shape[1] == LANES else weights[slot][:, 0:1]
            total = weight * value if total is None else total + weight * value
        return total

    def prepare(step):
        chain = own_slot
        decay = jnp.zeros((1, dwidth), F32)
        added = jnp.zeros((1, dwidth), F32)
        query = dec_q[step : step + 1, :]
        for t in range(step, -1, -1):
            value = jnp.exp2(decay) * pick(chain, vals, t)
            key = pick(chain, small, t)
            added = added + jnp.sum(key * query, axis=1, keepdims=True) * value
            decay = decay + pick(chain, vals, steps + t)
            if step == steps - 1:
                high = value.astype(BF16).astype(F32)
                dec_cv[t : t + 1, :] = high
                dec_cv[ROWS + t : ROWS + t + 1, :] = value - high
                dec_k[t : t + 1, :] = key
                dec_k[ROWS + t : ROWS + t + 1, :] = key
            if t > 0:
                parent = pick(chain, small, steps + t)
                chain = [jnp.where(parent == float(slot), 1.0, 0.0) for slot in range(nb)]
        open_now = pad[step : step + 1, 0:1]
        dec_d[step : step + 1, :] = jnp.exp2(decay)
        dec_add[step : step + 1, :] = added * open_now

    def rank_slots():
        score = [small[slot, 4 * steps : 4 * steps + 1, :] for slot in range(nb)]
        length = [small[slot, 4 * steps + 1 : 4 * steps + 2, :] for slot in range(nb)]
        for step in range(steps):
            new_score, new_length, normed = [], [], []
            for slot in range(nb):
                parent = small[slot, steps + step : steps + step + 1, :]
                picked_score, picked_length = score[0], length[0]
                for other in range(1, nb):
                    picked_score = jnp.where(parent == float(other), score[other], picked_score)
                    picked_length = jnp.where(parent == float(other), length[other], picked_length)
                new_score.append(picked_score + small[slot, 2 * steps + step : 2 * steps + step + 1, :])
                new_length.append(picked_length + small[slot, 3 * steps + step : 3 * steps + step + 1, :])
                normed.append(new_score[-1] / jnp.exp(0.6 * jnp.log((5.0 + new_length[-1]) / 6.0)))
            score, length = new_score, new_length
            best = functools.reduce(jnp.maximum, normed)
            mine = sum(own_slot[slot] * normed[slot] for slot in range(nb))
            rank_ref[:, step : step + 1] = (mine - best)[:, 0:1]

    def forward_down(k):
        for p in range(PIECES):
            dn_copy(dn_out, k, p).wait_recv()
            shrink = dn_recv[k, 0:1, :]
            rows = up_rows(p, ROWS)
            if p == 0:
                dn_out[k, 0:ROWS, :] = dn_recv[k, 0:ROWS, :] * own[k, 0:ROWS, :]
            dn_out[k, rows, :] = dn_recv[k, rows, :] + shrink * own[k, rows, :]
            dn_copy(dn_out, k, p).start()

    def finish(kk):
        at = lanes_of(kk)
        state = final[kk]
        read = mm(dec_q[...].astype(BF16), state.astype(BF16))
        keep = pad[:, 0:1]
        dec_add[:, at] = keep * (dec_d[:, at] * read) + dec_add[:, at]
        outer = mm_first(dec_cv[:, at].astype(BF16), dec_k[...].astype(BF16))
        beam_made[kk] = (state * dec_d[steps - 1 : steps, at]).T + outer
        beam_copy(kk).start()

    def await_and_finish(kk):
        @pl.when(b != owner)
        def _():
            f_copy(kk, 0).wait_recv()

        @pl.when(relays)
        def _():
            f_copy(kk, 0).start()

        finish(kk)

    up_lag = s * HOP
    dn_lag = (last - s) * HOP
    own_lag = jnp.maximum(jnp.maximum(up_lag, dn_lag), START + steps)
    first = lax.rem(s * dchunks, chunks)
    slots = chunks + max(last * HOP, START + steps) + SHARE

    def inside(k):
        return (k >= 0) & (k < chunks)

    def make_inner(k):
        values = x_ref[:, lanes_of(k)]
        for i in range(toks // LANES):
            at = slice(i * LANES, (i + 1) * LANES)
            until = (i + 1) * LANES
            made = []
            for j in range(PAIR):
                row = sums_ref[pl.ds(k * PAIR + j, 1), :]
                col = cols[k * PAIR + j, at, :]
                blocks = []
                for other in range(i + 1):
                    to = slice(other * LANES, (other + 1) * LANES)
                    gap = jnp.minimum(col - row[:, to], 0.0)
                    blocks.append((scores[at, to] * jnp.exp2(gap)).astype(BF16))
                weights = blocks[0] if i == 0 else jnp.concatenate(blocks, axis=1)
                made.append(mm(weights, values[0:until, :]))
            inner_ref[k, at, :] = jnp.where(left, made[0], made[1])

    def take_up(k):
        @pl.when(s == 0)
        def _():
            up_out[k] = own[k, ROWS : ROWS + n, :]
            out_made[k] = inner_ref[k].astype(BF16)
            out_copy(k).start()

        @pl.when(s > 0)
        def _():
            for p in range(PIECES):
                up_sent(k, p).wait_recv()
                up_out[k, up_rows(p), :] = (
                    own[k, 0:1, :] * up_recv[k, up_rows(p), :] + own[k, up_rows(p, ROWS), :]
                )

                @pl.when(s < last)
                def _():
                    up_sent(k, p).start()

            carried = mm(queries_ref[...], up_recv[k].astype(BF16)) * grown[k]
            out_made[k] = (inner_ref[k] + carried).astype(BF16)
            out_copy(k).start()

    def share_final(k):
        kk = place(k)

        @pl.when(s < last)
        def _():
            for p in range(PIECES):
                dn_copy(dn_out, k, p).wait_recv()
            final[kk] = dn_recv[k, 0:1, :] * up_out[k] + dn_recv[k, ROWS : ROWS + n, :]

        @pl.when(s == last)
        def _():
            final[kk] = up_out[k]

        for i in range(mates):
            f_copy(kk, i).start()

    def body(slot, carry):
        for step in range(steps):

            @pl.when(slot == START + step)
            def _():
                if step == 0:
                    for i in range(1, nb):
                        m_copy(i).wait_recv()
                        v_copy(i).wait_recv()
                prepare(step)

        starts = (slot < chunks) & (lax.rem(slot, together) == 0)

        @pl.when(starts & (s > 0) & (s < last))
        def _():
            for i in range(together):
                make_state(slot + i, 0)

        @pl.when(starts)
        def _():
            for i in range(together):
                make_inner(slot + i)

        down = slot - dn_lag
        goes_down = inside(down) & (s > target(down)) & (s < last)

        @pl.when(goes_down & (2 * s >= ns))
        def _():
            forward_down(down)

        @pl.when(inside(slot - up_lag))
        def _():
            take_up(slot - up_lag)

        @pl.when(goes_down & (2 * s < ns))
        def _():
            forward_down(down)

        at_end = slot - own_lag

        @pl.when(inside(at_end) & (s == target(at_end)))
        def _():
            share_final(at_end)

        kk = slot - own_lag - first - jnp.where(is_owner, 0, jnp.where(near, RELAY, SHARE))

        @pl.when((kk >= 0) & (kk < dchunks))
        def _():
            await_and_finish(kk)

        return carry

    lax.fori_loop(0, slots, body, 0)
    rank_slots()
    for step in range(steps):
        so_ref[:, step : step + 1, :] = dec_add[step : step + 1, :].astype(BF16)[None]

    for i in range(1, nb):
        m_copy(i).wait_send()
        v_copy(i).wait_send()

    def drain(k, carry):
        @pl.when(s < last)
        def _():
            for p in range(PIECES):
                up_sent(k, p).wait_send()

        @pl.when(s > target(k))
        def _():
            for p in range(PIECES):
                dn_copy(dn_out, k, p).wait_send()

        @pl.when(s == target(k))
        def _():
            for i in range(mates):
                f_copy(place(k), i).wait_send()

        return carry

    lax.fori_loop(0, chunks, drain, 0)

    def drain_results(k, carry):
        out_copy(k).wait()
        return carry

    lax.fori_loop(0, chunks, drain_results, 0)

    def drain_states(kk, carry):
        beam_copy(kk).wait()
        return carry

    lax.fori_loop(0, dchunks, drain_states, 0)

    @pl.when(relays)
    def _():
        def drain_relay(kk, carry):
            f_copy(kk, 0).wait_send()
            return carry

        lax.fori_loop(0, dchunks, drain_relay, 0)


def on_device(ns, nb, *args):
    x, keys, queries, decay, sv, sk, sq, sd, lp, par, fin, lens, score = args
    toks, width = x.shape
    n = keys.shape[1]
    heads = decay.shape[1]
    steps, _, dwidth = sv.shape
    chunks, dchunks = width // LANES, dwidth // LANES
    small_rows = -(-(4 * steps + 2) // ROWS) * ROWS
    dma = pltpu.SemaphoreType.DMA
    spec = pl.BlockSpec(memory_space=pltpu.VMEM)
    outside = pl.BlockSpec(memory_space=pl.ANY)
    peers = max(nb - 1, 1)
    turn = lambda a: jnp.transpose(a, (1, 0, 2))
    inputs = (x, keys, queries, decay.T, turn(sv), turn(sk), turn(sq), sd, lp.T, par.T, fin.T, lens, score)
    prompt, step_out, ranked, states = pl.pallas_call(
        functools.partial(kernel, ns, nb),
        out_shape=(
            jax.ShapeDtypeStruct((toks, width), BF16),
            jax.ShapeDtypeStruct((1, steps, dwidth), BF16),
            jax.ShapeDtypeStruct((1, steps), F32),
            jax.ShapeDtypeStruct((1, dwidth, n), F32),
        ),
        in_specs=[outside] * 13,
        out_specs=(outside, spec, spec, outside),
        scratch_shapes=[
            *[pltpu.VMEM(a.shape, a.dtype) for a in inputs[:11]],
            *[pltpu.SMEM(a.shape, a.dtype) for a in inputs[11:]],
            dma((len(inputs),)),
            pltpu.VMEM((heads, toks), F32),
            pltpu.VMEM((heads, toks, LANES), F32),
            pltpu.VMEM((chunks, toks, LANES), F32),
            pltpu.VMEM((n, toks), BF16),
            pltpu.VMEM((toks, toks), F32),
            pltpu.VMEM((chunks, n + ROWS, LANES), F32),
            pltpu.VMEM((chunks, toks, LANES), F32),
            pltpu.VMEM((chunks, n, LANES), F32),
            pltpu.VMEM((chunks, n, LANES), F32),
            pltpu.VMEM((chunks, n + ROWS, LANES), F32),
            pltpu.VMEM((chunks, n + ROWS, LANES), F32),
            pltpu.VMEM((dchunks, n, LANES), F32),
            pltpu.VMEM((nb, 2 * steps, dwidth), F32),
            pltpu.VMEM((nb, small_rows, LANES), F32),
            pltpu.VMEM((ROWS, LANES), F32),
            pltpu.VMEM((ROWS, dwidth), F32),
            pltpu.VMEM((ROWS, dwidth), F32),
            pltpu.VMEM((2 * ROWS, dwidth), F32),
            pltpu.VMEM((2 * ROWS, n), F32),
            pltpu.VMEM((ROWS, n), F32),
            dma((chunks, PIECES)),
            dma((chunks, PIECES)),
            dma((chunks, PIECES)),
            dma((chunks, PIECES)),
            dma((dchunks, nb // CORES)),
            dma((dchunks,)),
            dma((peers,)),
            dma((peers,)),
            dma((peers,)),
            dma((peers,)),
            pltpu.VMEM((chunks, toks, LANES), BF16),
            pltpu.VMEM((dchunks, LANES, n), F32),
            dma((chunks,)),
            dma((dchunks,)),
        ],
        compiler_params=pltpu.CompilerParams(
            collective_id=0, has_side_effects=True, vmem_limit_bytes=60 * 1024 * 1024
        ),
    )(*inputs)
    return prompt, turn(step_out), ranked.T, states


def solution(mesh):
    return jax.shard_map(
        functools.partial(on_device, mesh.shape["seq"], mesh.shape["beam"]),
        mesh=mesh,
        in_specs=(
            P(("groups", "seq"), "beam"),
            P(("groups", "seq"), None),
            P(("groups", "seq"), None),
            P(("groups", "seq"), "beam"),
            P("groups", "beam", "seq"),
            P("groups", "beam", None),
            P("groups", "beam", None),
            P("groups", "beam", "seq"),
            P("groups", "beam"),
            P("groups", "beam"),
            P("groups", "beam"),
            P(("groups", "beam")),
            P(("groups", "beam")),
        ),
        out_specs=(
            P(("groups", "seq"), "beam"),
            P("groups", "beam", "seq"),
            P("groups", "beam"),
            P(("groups", "beam"), "seq", None),
        ),
        check_vma=False,
    )
```
